256 devices in a mesh: pair: 32 (over z, y), fock: 8 (over x, core).
Axes of the slice: x: 4, y: 4, z: 8, core: 2. Of those that a mesh axis runs over, the one named last changes fastest.
Arguments:
- geminal: bfloat16 [32, 12288, 128], P('pair', 'fock'), may hold values from -9 to 9
- fock_matrix: bfloat16 [8, 32, 48, 12288], P(None, 'pair', None, 'fock'), as said below
- slot_occupied_pair: int32 [32], replicated, may hold values from 0 to 1
- slot_column_block: int32 [32], replicated, may hold values from 0 to 7
- slot_live: int32 [32], replicated, may hold values from 0 to 1, as said below
Outputs:
- fock_geminal: bfloat16 [32, 12288, 128], P(None, ('fock', 'pair'))
- bmat: float32 [2, 2], replicated
The draws below stay inside these ranges and needn't reach their ends.
Inputs may be any that keep to these rules, and one draw needn't show every extreme that they name: `slot_live`: exactly 24 slots are 1. `fock_matrix`: the matrix read as in the first step is symmetric.
All inputs are finite; a program needn't handle non-finite values.
Results may differ from the reference program's by a relative error of at most 0.001.
Values may be sent and summed in bfloat16 or wider, within the bound.
No kernel may reach another device: no remote copies, remote signals or barrier semaphores. Data moves between devices by JAX's collectives and lax.ppermute only.
A program may use at most 128 MiB of HBM per device.

```python
import math
import jax
import jax.numpy as jnp
from jax import lax

ORBITAL_SPAN = 12288
BLOCK_WIDTH = 128
SLOT_COUNT = 32
NLIVE = 24
COLUMN_BLOCKS = 96
ROWS_DEV = 48
N_PAIR = 32
N_FOCK = 8


def draw_geminal(key, part):
    key = jax.random.fold_in(key, 5)
    key_amp, key_noise = jax.random.split(key)
    position = jnp.arange(ORBITAL_SPAN, dtype=jnp.float32) / ORBITAL_SPAN
    growth = jnp.exp(0.35 * position)[None, :, None]
    amplitude = jax.random.uniform(key_amp, (BLOCK_WIDTH,), jnp.float32, 0.4, 0.8)
    noise_draw = jnp.clip(jax.random.normal(key_noise, (SLOT_COUNT, ORBITAL_SPAN, BLOCK_WIDTH), jnp.float32), -5.0, 5.0)
    values = growth * (amplitude[None, None, :] + noise_draw)
    return values.astype(jnp.bfloat16)


def draw_fock_matrix(key, part):
    key = jax.random.fold_in(key, 7)
    key_levels, key_noise = jax.random.split(key)
    position = jnp.arange(ORBITAL_SPAN, dtype=jnp.float32) / ORBITAL_SPAN
    rough = jnp.exp(jax.random.uniform(key_levels, (ORBITAL_SPAN,), jnp.float32, 0.0, math.log(2.0)))
    levels = 0.5 * jnp.exp(math.log(4.0) * position) * rough
    noise_draw = jax.random.normal(key_noise, (ORBITAL_SPAN, ORBITAL_SPAN), jnp.float32)
    coupling = (noise_draw + noise_draw.T) * (1.0 / math.sqrt(2.0 * ORBITAL_SPAN)) + 2.0 / ORBITAL_SPAN
    full_matrix = coupling + jnp.diag(levels)
    return full_matrix.T.reshape(N_FOCK, N_PAIR, ROWS_DEV, ORBITAL_SPAN).astype(jnp.bfloat16)


def draw_slot_live(key, part):
    key = jax.random.fold_in(key, 11)
    slot_ordering = jax.random.permutation(key, SLOT_COUNT)
    return (slot_ordering < NLIVE).astype(jnp.int32)


def with_ends(drawn, stream_key, least, largest):
    spot = [jax.random.randint(jax.random.fold_in(stream_key, axis), (), 0, length) for axis, length in enumerate(drawn.shape)]
    main_axis = drawn.shape.index(max(drawn.shape))
    beside = spot[:main_axis] + [(spot[main_axis] + 1) % drawn.shape[main_axis]] + spot[main_axis + 1:]
    return drawn.at[tuple(spot)].set(least).at[tuple(beside)].set(largest)


def setup_inputs(seed: int = 0) -> dict:
    splits = jax.random.split(jax.random.key(seed), 6)
    return {
        "geminal": draw_geminal(jax.random.fold_in(splits[5], 71), 0),
        "fock_matrix": draw_fock_matrix(jax.random.fold_in(splits[5], 71), 0),
        "slot_occupied_pair": with_ends(jax.random.randint(splits[2], (SLOT_COUNT,), 0, 2), jax.random.fold_in(splits[2], 1), 0, 1).astype(jnp.int32),
        "slot_column_block": with_ends(jax.random.randint(splits[3], (SLOT_COUNT,), 0, min(COLUMN_BLOCKS, SLOT_COUNT // 4)), jax.random.fold_in(splits[3], 1), 0, (min(COLUMN_BLOCKS, SLOT_COUNT // 4)) - 1).astype(jnp.int32),
        "slot_live": draw_slot_live(jax.random.fold_in(splits[5], 71), 0),
    }


HIGHEST = lax.Precision.HIGHEST


def reference(geminal, fock_matrix, slot_occupied_pair, slot_column_block, slot_live):
    fock_full = fock_matrix.reshape(ORBITAL_SPAN, ORBITAL_SPAN).T.astype(jnp.float32)
    alive_mask = slot_live.astype(jnp.float32)

    def weighted_block(packed):
        gem_block, alive_flag = packed
        product = jnp.dot(fock_full, gem_block.astype(jnp.float32), precision=HIGHEST)
        return (product * alive_flag).astype(jnp.bfloat16)

    fock_geminal = lax.map(weighted_block, (geminal, alive_mask))
    intersections = jnp.einsum("kpb,lpb->kl", geminal.astype(jnp.float32), fock_geminal.astype(jnp.float32), precision=HIGHEST)
    same_block = (slot_column_block[:, None] == slot_column_block[None, :]).astype(jnp.float32)
    matching = alive_mask[:, None] * alive_mask[None, :] * same_block
    onehot = (slot_occupied_pair[:, None] == jnp.arange(2, dtype=jnp.int32)[None, :]).astype(jnp.float32)
    inner = jnp.dot(onehot.T, matching * intersections, precision=HIGHEST)
    bmat = jnp.dot(inner, onehot, precision=HIGHEST) / (ORBITAL_SPAN * BLOCK_WIDTH)
    return fock_geminal, bmat
```

```python
import jax
import jax.numpy as jnp
from jax import lax
from jax.sharding import PartitionSpec as P

HIGHEST = lax.Precision.HIGHEST
NZ, NY, NX, NC = 8, 4, 4, 2


def shift_z(v, s):
    return lax.ppermute(
        v, "pair", [(z * NY + y, (z + s) % NZ * NY + y) for z in range(NZ) for y in range(NY)]
    )


def shift_y(v, s):
    return lax.ppermute(
        v, "pair", [(z * NY + y, z * NY + (y + s) % NY) for z in range(NZ) for y in range(NY)]
    )


def shift_x(v, s):
    return lax.ppermute(
        v, "fock", [(x * NC + c, (x + s) % NX * NC + c) for x in range(NX) for c in range(NC)]
    )


def swap_core(v):
    return lax.ppermute(
        v, "fock", [(x * NC + c, x * NC + 1 - c) for x in range(NX) for c in range(NC)]
    )


def total_over(v, axis):
    n = lax.axis_size(axis)
    return lax.all_to_all(jnp.broadcast_to(v, (n,) + v.shape), axis, 0, 0).sum(0)


def gather_z(g):
    half = g.shape[0] // 2
    parts = []
    for h, piece in enumerate((g[:half], g[half:])):
        right, left = [piece], [piece]
        for _ in range(3):
            right.append(shift_z(right[-1], 1))
            left.append(shift_z(left[-1], -1))
        far = shift_z(right[3], 1) if h == 0 else shift_z(left[3], -1)
        parts.append([piece, left[1], left[2], left[3], far, right[3], right[2], right[1]])
    return parts


def panel_total(away, keep):
    total = keep + swap_core(away)
    half = total.shape[1] // 2
    from_left = shift_x(total[2, :half], 1)
    from_right = shift_x(total[2, half:], -1)
    to_right = total[1].at[:half].add(from_left)
    to_left = total[3].at[half:].add(from_right)
    return total[0] + shift_x(to_right, 1) + shift_x(to_left, -1)


def on_device(geminal, fock_matrix, slot_occupied_pair, slot_column_block, slot_live):
    n_fock, _, width, panel_rows = fock_matrix.shape
    columns = geminal.shape[2]
    pair_at, fock_at = lax.axis_index("pair"), lax.axis_index("fock")
    z, y = pair_at // NY, pair_at % NY
    x, c = fock_at // NC, fock_at % NC

    by_chip = fock_matrix.reshape(NX, NC, width, panel_rows)
    by_chip = jnp.roll(by_chip, (-x, -c), (0, 1))
    keep, away = by_chip[:, 0], by_chip[:, 1]
    keep_left, away_left = shift_y(keep, 1), shift_y(away, 1)
    keep_right, away_right = shift_y(keep, -1), shift_y(away, -1)
    away_far, keep_far = shift_y(away_left, 1), shift_y(keep_right, -1)

    parts = gather_z(geminal[0])
    held = jnp.concatenate([jnp.concatenate(p, axis=1) for p in parts], axis=0)

    def live_of(v):
        return jnp.roll(v.reshape(NZ, NY), (-z, -y), (0, 1)).T.reshape(-1)

    alive = live_of(slot_live).astype(jnp.float32)
    block = live_of(slot_column_block)
    occupied = live_of(slot_occupied_pair)
    own_alive = jnp.repeat(alive.reshape(NY, NZ)[0], columns)

    def chunk(away_rows, keep_rows):
        def product(rows):
            flat = rows.reshape(NX * width, panel_rows)
            out = jnp.dot(flat, held, preferred_element_type=jnp.float32)
            return out.reshape(NX, width, -1)

        total = panel_total(product(away_rows), product(keep_rows))
        return (total * own_alive[None, :]).astype(jnp.bfloat16)

    sources = {0: (away, keep), -1: (away_left, keep_left), 1: (away_right, keep_right), 2: (away_far, keep_far)}
    made, rows_of = {}, {}
    for d, (a, k) in sources.items():
        owner = z * NY + (y + d) % NY
        own = lax.dynamic_slice_in_dim(held, owner * width, width, 0)
        out = chunk(a, k)
        rows_of[-d % NY] = shift_y(own, d) if d else own
        made[-d % NY] = shift_y(out, d) if d else out
    left_rows = jnp.stack([rows_of[i] for i in range(NY)]).reshape(NY, width, NZ, columns)
    right_rows = jnp.stack([made[i] for i in range(NY)]).reshape(NY, width, NZ, columns)

    n_slots = NZ * NY
    intersections = jnp.einsum(
        "kweb,lwfb->kelf", left_rows, right_rows, preferred_element_type=jnp.float32
    ).reshape(n_slots, n_slots)
    same_block = (block[:, None] == block[None, :]).astype(jnp.float32)
    matching = alive[:, None] * alive[None, :] * same_block
    onehot = (occupied[:, None] == jnp.arange(2, dtype=jnp.int32)[None, :]).astype(jnp.float32)
    inner = jnp.dot(onehot.T, matching * intersections, precision=HIGHEST)
    normalizer = 1.0 / (panel_rows * n_fock * columns)
    bmat = jnp.dot(inner, onehot, precision=HIGHEST) * normalizer
    spread = jnp.pad(bmat.reshape(1, 4), ((0, 0), (0, 124)))
    spread = total_over(total_over(spread, "pair"), "fock")
    bmat = spread[0, :4].reshape(2, 2)

    ordered = right_rows.transpose(2, 0, 1, 3)
    ordered = jnp.roll(ordered, (z, y), (0, 1))
    return ordered.reshape(n_slots, width, columns), bmat


def solution(mesh):
    return jax.shard_map(
        on_device,
        mesh=mesh,
        in_specs=(P("pair", "fock", None), P(None, "pair", None, "fock"), P(), P(), P()),
        out_specs=(P(None, ("fock", "pair"), None), P()),
        check_vma=False,
    )
```

```python
import functools

import jax
import jax.numpy as jnp
from jax import lax
from jax.experimental import pallas as pl
from jax.experimental.pallas import tpu as pltpu
from jax.sharding import PartitionSpec as P

HIGHEST = lax.Precision.HIGHEST
NZ, NY, NX, NC = 8, 4, 4, 2
SAME_CORE = [[x * NC + c for x in range(NX)] for c in range(NC)]

VMEM = pl.BlockSpec(memory_space=pltpu.VMEM)
SMEM = pl.BlockSpec(memory_space=pltpu.SMEM)
ANY = pl.BlockSpec(memory_space=pl.ANY)
CHEAP = pl.CostEstimate(flops=1, bytes_accessed=1, transcendentals=0)

NEAR, FAR = (0, 1, 7, 2, 6), (3, 5, 4)
ORDER = NEAR + FAR
FIRST = ((0, NEAR), (1, NEAR))
SECOND = ((0, FAR), (1, FAR), (2, ORDER), (3, ORDER))


def offset(j, x):
    return (0, -1, 1, 2)[j] if x < NX // 2 else (0, 1, -1, 2)[j]


def shift_z(v, s):
    return lax.ppermute(
        v, "pair", [(z * NY + y, (z + s) % NZ * NY + y) for z in range(NZ) for y in range(NY)]
    )


def shift_y(v, s):
    return lax.ppermute(
        v, "pair", [(z * NY + y, z * NY + (y + s) % NY) for z in range(NZ) for y in range(NY)]
    )


def to_owner(v, j):
    moves = []
    for z in range(NZ):
        for y in range(NY):
            for x in range(NX):
                for c in range(NC):
                    to = z * NY + (y + offset(j, x)) % NY
                    moves.append(((z * NY + y) * NX * NC + x * NC + c, to * NX * NC + x * NC + c))
    return lax.ppermute(v, ("pair", "fock"), moves) if j else v


def swap_core(v):
    return lax.ppermute(
        v, "fock", [(x * NC + c, x * NC + 1 - c) for x in range(NX) for c in range(NC)]
    )


def total_over(v, axis):
    n = lax.axis_size(axis)
    return lax.all_to_all(jnp.broadcast_to(v, (n,) + v.shape), axis, 0, 0).sum(0)


def split_kernel(own_ref, low_ref, high_ref):
    half = own_ref.shape[0] // 2
    low_ref[...] = own_ref[:half]
    high_ref[...] = own_ref[half:]


def split(own):
    half = jax.ShapeDtypeStruct((own.shape[0] // 2,) + own.shape[1:], own.dtype)
    return pl.pallas_call(
        split_kernel,
        out_shape=[half, half],
        in_specs=[VMEM],
        out_specs=[VMEM] * 2,
        compiler_params=pltpu.CompilerParams(vmem_limit_bytes=8 * 2**20),
        cost_estimate=CHEAP,
    )(own)


def join_kernel(low_ref, high_ref, left_ref, right_ref, to_right_ref, to_left_ref):
    half = low_ref.shape[0]
    to_right_ref[:half] = left_ref[...]
    to_right_ref[half:] = high_ref[...]
    to_left_ref[:half] = low_ref[...]
    to_left_ref[half:] = right_ref[...]


def join(low, high, left, right):
    whole = jax.ShapeDtypeStruct((2 * low.shape[0],) + low.shape[1:], low.dtype)
    return pl.pallas_call(
        join_kernel,
        out_shape=[whole, whole],
        in_specs=[VMEM] * 4,
        out_specs=[VMEM] * 2,
        compiler_params=pltpu.CompilerParams(vmem_limit_bytes=12 * 2**20),
        cost_estimate=CHEAP,
    )(low, high, left, right)


def pack_kernel(keep_ref, recv_ref, out_ref):
    _, width, total = keep_ref.shape
    columns = out_ref.shape[2] - total
    lane = lax.broadcasted_iota(jnp.int32, (width, columns), 1)
    exponents = jnp.zeros((width, columns), jnp.int32)
    for u in range(total // columns):
        span = slice(u * columns, (u + 1) * columns)
        value = keep_ref[0, :, span] + recv_ref[0, :, span]
        top = jnp.maximum(jnp.max(jnp.abs(value), axis=1, keepdims=True), 2.0**-100)
        power = jnp.ceil(jnp.log2(top)) - 15.0
        scaled = jnp.clip(jnp.round(value * jnp.exp2(-power)), -32767.0, 32767.0)
        out_ref[0, :, span] = scaled.astype(jnp.int32).astype(jnp.int16)
        exponents = jnp.where(lane == u, power.astype(jnp.int32), exponents)
    out_ref[0, :, total:] = exponents.astype(jnp.int16)


def pack(keep, recv, columns):
    n, width, total = keep.shape
    return pl.pallas_call(
        pack_kernel,
        out_shape=jax.ShapeDtypeStruct((n, width, total + columns), jnp.int16),
        grid=(n,),
        in_specs=[pl.BlockSpec((1, width, total), lambda t: (t, 0, 0))] * 2,
        out_specs=pl.BlockSpec((1, width, total + columns), lambda t: (t, 0, 0)),
        compiler_params=pltpu.CompilerParams(vmem_limit_bytes=16 * 2**20),
        cost_estimate=CHEAP,
    )(keep, recv)


def products_kernel(plan, n_f, g_rows, at_ref, *refs):
    n_g = sum(len(r) for r in g_rows)
    f_refs, g_refs = refs[:n_f], list(refs[n_f : n_f + n_g])
    away_ref, keep_ref, *rows_ref, joined = refs[n_f + n_g :]
    columns = g_refs[0].shape[1]
    first_core = at_ref[0] == 0
    for j, rows in enumerate(g_rows):
        at = 0
        for n in rows:
            joined[at : at + n, j * columns : (j + 1) * columns] = g_refs.pop(0)[...]
            at += n
    for ref in rows_ref:
        count = ref.shape[0]
        ref[...] = joined[pl.ds(pl.multiple_of(at_ref[1] * count, 64), count), :]
    at = 0
    for pieces, lo, hi in plan:
        span = (hi - lo) * columns
        parts = []
        for i, part in pieces:
            n, cores, width, depth = f_refs[i].shape
            value = f_refs[i][...] if part is None else f_refs[i][part * (n // 2) : (part + 1) * (n // 2)]
            parts.append(value.reshape(-1, depth))
        lhs = parts[0] if len(parts) == 1 else jnp.concatenate(parts, axis=0)
        out = jnp.dot(lhs, joined[:, lo * columns : hi * columns], preferred_element_type=jnp.float32)
        out = out.reshape(NX, NC, width, span)
        keep_ref[:, :, at : at + span] = jnp.where(first_core, out[:, 0], out[:, 1])
        away_ref[:, :, at : at + span] = jnp.where(first_core, out[:, 1], out[:, 0])
        at += span


def products(plan, at, f_arrays, g_pieces, with_rows):
    width, rows = f_arrays[0].shape[2:]
    g_rows = tuple(tuple(v.shape[0] for v in slot) for slot in g_pieces)
    g_flat = [v for slot in g_pieces for v in slot]
    columns = g_flat[0].shape[1]
    units = sum(hi - lo for _, lo, hi in plan)
    terms = jax.ShapeDtypeStruct((NX, width, units * columns), jnp.float32)
    own = jax.ShapeDtypeStruct((NY * width, len(g_pieces) * columns), jnp.bfloat16)
    return pl.pallas_call(
        functools.partial(products_kernel, plan, len(f_arrays), g_rows),
        out_shape=[terms, terms] + [own] * with_rows,
        in_specs=[SMEM] + [VMEM] * (len(f_arrays) + len(g_flat)),
        out_specs=[VMEM] * (2 + with_rows),
        scratch_shapes=[pltpu.VMEM((rows, len(g_pieces) * columns), jnp.bfloat16)],
        compiler_params=pltpu.CompilerParams(vmem_limit_bytes=28 * 2**20),
        cost_estimate=CHEAP,
    )(at, *f_arrays, *g_flat)


def unpack_into(total_ref, mask_ref, plan, done_refs, held, arrived):
    n, width, _ = total_ref.shape
    columns = mask_ref.shape[1] // NZ
    copies = [pltpu.make_async_copy(total_ref.at[t], held.at[t], arrived.at[t]) for t in range(n)]
    for copy in copies:
        copy.start()
    for copy in copies:
        copy.wait()
    units = held.shape[2] - columns
    scales = [jnp.exp2(held[t, :, units:].astype(jnp.int32).astype(jnp.float32)) for t in range(n)]
    made, u = [], 0
    for done_ref, (_, es) in zip(done_refs, plan):
        for i, e in enumerate(es):
            value = 0.0
            for t in range(n):
                term = held[t, :, u * columns : (u + 1) * columns].astype(jnp.int32).astype(jnp.float32)
                value = value + term * scales[t][:, u : u + 1]
            rounded = (value * mask_ref[:, e * columns : (e + 1) * columns]).astype(jnp.bfloat16)
            done_ref[:, i * columns : (i + 1) * columns] = rounded
            u += 1


def dots_into(plan, at_ref, done_refs, weight_ref, row_refs, bmat_ref, dots):
    width = done_refs[0].shape[0]
    columns = dots.shape[1]
    starts = [pl.multiple_of(at_ref[j] * width, 16) for j, _ in plan]
    count = {e for _, es in plan for e in es}
    if len(count) < NZ:
        dots[...] = jnp.zeros_like(dots)
    for k in range(NY):
        for f in range(NZ):
            sums = {}
            for (_, es), start, done_ref in zip(plan, starts, done_refs):
                row = row_refs[k][pl.ds(start, width), f * columns : (f + 1) * columns].astype(jnp.float32)
                for i, e in enumerate(es):
                    term = row * done_ref[:, i * columns : (i + 1) * columns].astype(jnp.float32)
                    term = term.reshape(width // 8, 8, columns).sum(0)
                    sums[e] = sums[e] + term if e in sums else term
            for e, term in sums.items():
                i = (k * NZ + f) * NZ + e
                dots[i : i + 1] = term.sum(0, keepdims=True)
    bmat_ref[...] = (dots[...].sum(1, keepdims=True) * weight_ref[...]).sum(0, keepdims=True)


def early_kernel(plan, total_ref, mask_ref, *refs):
    *done_refs, held, arrived = refs
    unpack_into(total_ref, mask_ref, plan, done_refs, held, arrived)


def early_dots_kernel(plan, at_ref, weight_ref, *refs):
    n = len(plan)
    dots_into(plan, at_ref, refs[:n], weight_ref, refs[n : n + NY], refs[n + NY], refs[n + NY + 1])


def late_kernel(plan, at_ref, total_ref, mask_ref, weight_ref, bmat_in_ref, *refs):
    row_refs, refs = refs[:NY], refs[NY:]
    *done_refs, bmat_ref, held, arrived, dots = refs
    unpack_into(total_ref, mask_ref, plan, done_refs, held, arrived)
    dots_into(plan, at_ref, done_refs, weight_ref, row_refs, bmat_ref, dots)
    bmat_ref[...] += bmat_in_ref[...]


def done_shapes(plan, width, columns):
    return [jax.ShapeDtypeStruct((width, len(es) * columns), jnp.bfloat16) for _, es in plan]


def early_finish(plan, total, mask):
    return pl.pallas_call(
        functools.partial(early_kernel, plan),
        out_shape=done_shapes(plan, total.shape[1], mask.shape[1] // NZ),
        in_specs=[ANY, VMEM],
        out_specs=[VMEM] * len(plan),
        scratch_shapes=[pltpu.VMEM(total.shape, total.dtype), pltpu.SemaphoreType.DMA((total.shape[0],))],
        compiler_params=pltpu.CompilerParams(vmem_limit_bytes=16 * 2**20),
        cost_estimate=CHEAP,
    )(total, mask)


def early_dots(plan, at, weight, done, rows):
    columns = rows[0].shape[1] // NZ
    return pl.pallas_call(
        functools.partial(early_dots_kernel, plan),
        out_shape=jax.ShapeDtypeStruct((1, weight.shape[1]), jnp.float32),
        in_specs=[SMEM] + [VMEM] * (1 + len(done) + NY),
        out_specs=VMEM,
        scratch_shapes=[pltpu.VMEM((NY * NZ * NZ, columns), jnp.float32)],
        compiler_params=pltpu.CompilerParams(vmem_limit_bytes=16 * 2**20),
        cost_estimate=CHEAP,
    )(at, weight, *done, *rows)


def late_finish(plan, at, total, mask, weight, bmat, rows):
    columns = rows[0].shape[1] // NZ
    return pl.pallas_call(
        functools.partial(late_kernel, plan),
        out_shape=done_shapes(plan, total.shape[1], columns)
        + [jax.ShapeDtypeStruct((1, weight.shape[1]), jnp.float32)],
        in_specs=[SMEM, ANY] + [VMEM] * (3 + NY),
        out_specs=[VMEM] * (len(plan) + 1),
        scratch_shapes=[
            pltpu.VMEM(total.shape, total.dtype),
            pltpu.SemaphoreType.DMA((total.shape[0],)),
            pltpu.VMEM((NY * NZ * NZ, columns), jnp.float32),
        ],
        compiler_params=pltpu.CompilerParams(vmem_limit_bytes=16 * 2**20),
        cost_estimate=CHEAP,
    )(at, total, mask, weight, bmat, *rows)


def place_kernel(plan, at_ref, *refs):
    *piece_refs, out_ref = refs
    columns = out_ref.shape[2]
    for piece_ref, (k, es) in zip(piece_refs, plan):
        for j, e in enumerate(es):
            slot = lax.rem(at_ref[0] + e, NZ) * NY + at_ref[1 + k]
            out_ref[slot] = piece_ref[:, j * columns : (j + 1) * columns]


def place(plan, at, pieces, columns):
    width = pieces[0].shape[0]
    return pl.pallas_call(
        functools.partial(place_kernel, plan),
        out_shape=jax.ShapeDtypeStruct((NZ * NY, width, columns), jnp.bfloat16),
        in_specs=[SMEM] + [VMEM] * len(pieces),
        out_specs=VMEM,
        compiler_params=pltpu.CompilerParams(vmem_limit_bytes=8 * 2**20),
        cost_estimate=CHEAP,
    )(at, *pieces)


def on_device(geminal, fock_matrix, slot_occupied_pair, slot_column_block, slot_live):
    n_fock, _, width, panel_rows = fock_matrix.shape
    columns = geminal.shape[2]
    n_slots = NZ * NY
    pair_at, fock_at = lax.axis_index("pair"), lax.axis_index("fock")
    z, y = pair_at // NY, pair_at % NY
    at = jnp.stack([fock_at % NC, z])

    own = fock_matrix.reshape(NX, NC, width, panel_rows)
    low, high = split(own)
    g, low, high = lax.optimization_barrier((geminal[0], low, high))
    from_left, from_right = shift_y(low, 1), shift_y(high, -1)
    to_right, to_left = join(low, high, from_left, from_right)
    after_left, after_right = shift_y(to_right, 1), shift_y(to_left, -1)
    f_arrays = [own, from_left, from_right, after_left, after_right]
    f_blocks = (((0, None),), ((1, None), (2, None)), ((4, 0), (3, 1)), ((3, 0), (4, 1)))

    half = panel_rows // 2
    slots = {0: g}
    slots[1], slots[7] = shift_z(slots[0], -1), shift_z(slots[0], 1)
    slots[2], slots[6] = shift_z(slots[1], -1), shift_z(slots[7], 1)
    slots[3], slots[5] = shift_z(slots[2], -1), shift_z(slots[6], 1)
    slots = {e: [v] for e, v in slots.items()}

    at_z = (z + jnp.array(ORDER, jnp.int32)) % NZ
    at_y = (y - jnp.arange(NY, dtype=jnp.int32)) % NY
    index = (at_z[None, :] * NY + at_y[:, None]).reshape(-1)
    chosen = (index[:, None] == jnp.arange(n_slots, dtype=jnp.int32)[None, :]).astype(jnp.float32)
    facts = jnp.stack([slot_live, slot_column_block, slot_occupied_pair], axis=1).astype(jnp.float32)
    facts = jnp.dot(chosen, facts, precision=HIGHEST)
    alive, block, occupied = facts[:, 0], facts[:, 1], facts[:, 2]
    matching = alive[:, None] * alive[None, :NZ] * (block[:, None] == block[None, :NZ])
    normalizer = 1.0 / (panel_rows * n_fock * columns)
    entry = 2 * occupied[:, None] + occupied[None, :NZ]
    entries = jnp.arange(128, dtype=jnp.float32)
    weight = (matching[:, :, None] * normalizer * (entry[:, :, None] == entries)).reshape(-1, 128)
    mask = jnp.repeat(alive[:NZ], columns).reshape(1, -1)

    x = fock_at // NC
    sign = jnp.where(x < NX // 2, -1, 1)
    steps = jnp.stack([0 * sign, sign, -sign, 0 * sign + 2])
    rows_at, classes = (y + steps) % NY, (y - steps) % NY

    def start(plan, order, arrays, with_rows):
        plan = tuple((f_blocks[j], order.index(es[0]), order.index(es[0]) + len(es)) for j, es in plan)
        away, *rest = products(plan, at, arrays, [slots[e] for e in order], with_rows)
        return swap_core(away), *rest

    def spread(total):
        return lax.all_to_all(total, "fock", 0, 0, axis_index_groups=SAME_CORE)

    def places(plan):
        return tuple((j, tuple(ORDER.index(e) for e in es)) for j, es in plan)

    def owned(plan, done):
        return [to_owner(v, j) for (j, _), v in zip(plan, done)]

    first = lax.optimization_barrier((*f_arrays[:3], to_right, to_left))[:3]
    recv, keep = start(FIRST, NEAR, list(first), 0)
    packed = pack(keep, recv, columns)
    slots[3], slots[5], packed = lax.optimization_barrier((slots[3], slots[5], packed))
    slots[4] = [shift_z(slots[3][0][:half], -1), shift_z(slots[5][0][half:], 1)]
    early = spread(packed)
    *f_arrays, early = lax.optimization_barrier((*f_arrays, early))
    done = early_finish(places(FIRST), early, mask)
    moved = owned(FIRST, done)
    recv, keep, joined = start(SECOND, ORDER, f_arrays, 1)
    rows = [joined, shift_y(joined, 1), shift_y(joined, 2), shift_y(joined, -1)]
    late = spread(pack(keep, recv, columns))
    bmat = early_dots(places(FIRST), rows_at, weight, done, rows)
    *done, bmat = late_finish(places(SECOND), rows_at, late, mask, weight, bmat, rows)
    more = owned(SECOND, done)
    bmat = total_over(bmat, "pair")

    at_place = jnp.concatenate([z.reshape(1), classes])
    *pieces, bmat = lax.optimization_barrier((*moved, *more, bmat))
    out = place(FIRST + SECOND, at_place, pieces, columns)
    return out, total_over(bmat, "fock")[0, :4].reshape(2, 2)


def solution(mesh):
    return jax.shard_map(
        on_device,
        mesh=mesh,
        in_specs=(P("pair", "fock", None), P(None, "pair", None, "fock"), P(), P(), P()),
        out_specs=(P(None, ("fock", "pair"), None), P()),
        check_vma=False,
    )
```

```python
import functools

import jax
import jax.numpy as jnp
from jax import lax
from jax.experimental import pallas as pl
from jax.experimental.pallas import tpu as pltpu
from jax.sharding import Mesh
from jax.sharding import PartitionSpec as P

HIGHEST = lax.Precision.HIGHEST
NZ, NY, NX, NC = 8, 4, 4, 2
VMEM = pl.BlockSpec(memory_space=pltpu.VMEM)
SMEM = pl.BlockSpec(memory_space=pltpu.SMEM)
ANY = pl.BlockSpec(memory_space=pl.ANY)
CHEAP = pl.CostEstimate(flops=1, bytes_accessed=1, transcendentals=0)

NEAR, FAR = (0, 1, 7), (2, 6, 3, 5, 4)
ORDER = NEAR + FAR
FIRST = ((0, NEAR), (1, NEAR))
SECOND = ((0, FAR), (1, FAR), (2, ORDER), (3, ORDER))


def offset(j, x):
    return (0, -1, 1, 2)[j] if x < NX // 2 else (0, 1, -1, 2)[j]


def offset_at(j, x):
    near, far = jnp.where(x < NX // 2, NY - 1, 1), jnp.where(x < NX // 2, 1, NY - 1)
    return (0, near, far, 2)[j]


def shift_z(v, s):
    return lax.ppermute(v, "z", [(z, (z + s) % NZ) for z in range(NZ)])


def shift_y(v, s):
    return lax.ppermute(v, "y", [(y, (y + s) % NY) for y in range(NY)])


def to_owner(v, j):
    moves = []
    for y in range(NY):
        for x in range(NX):
            moves.append((y * NX + x, (y + offset(j, x)) % NY * NX + x))
    return lax.ppermute(v, ("y", "x"), moves) if j else v


def swap_core(v):
    return lax.ppermute(v, "c", [(0, 1), (1, 0)])


def total_over(v, axis, n):
    return lax.all_to_all(jnp.broadcast_to(v, (n,) + v.shape), axis, 0, 0).sum(0)


def split_kernel(own_ref, low_ref, high_ref):
    half = own_ref.shape[0] // 2
    low_ref[...] = own_ref[:half]
    high_ref[...] = own_ref[half:]


def split(own):
    half = jax.ShapeDtypeStruct((own.shape[0] // 2,) + own.shape[1:], own.dtype)
    return pl.pallas_call(
        split_kernel,
        out_shape=[half, half],
        in_specs=[VMEM],
        out_specs=[VMEM] * 2,
        compiler_params=pltpu.CompilerParams(vmem_limit_bytes=8 * 2**20),
        cost_estimate=CHEAP,
    )(own)


def join_kernel(low_ref, high_ref, left_ref, right_ref, to_right_ref, to_left_ref):
    half = low_ref.shape[0]
    to_right_ref[:half] = left_ref[...]
    to_right_ref[half:] = high_ref[...]
    to_left_ref[:half] = low_ref[...]
    to_left_ref[half:] = right_ref[...]


def join(low, high, left, right):
    whole = jax.ShapeDtypeStruct((2 * low.shape[0],) + low.shape[1:], low.dtype)
    return pl.pallas_call(
        join_kernel,
        out_shape=[whole, whole],
        in_specs=[VMEM] * 4,
        out_specs=[VMEM] * 2,
        compiler_params=pltpu.CompilerParams(vmem_limit_bytes=12 * 2**20),
        cost_estimate=CHEAP,
    )(low, high, left, right)


def pack_kernel(keep_ref, recv_ref, *refs):
    *before_ref, out_ref = refs
    _, width, total = keep_ref.shape
    columns = 128
    lane = lax.broadcasted_iota(jnp.int32, (width, columns), 1)
    at = 0
    exponents = jnp.zeros((width, columns), jnp.int32)
    for ref in before_ref:
        at = ref.shape[2] - columns
        out_ref[0, :, :at] = ref[0, :, :at]
        exponents = ref[0, :, at:].astype(jnp.int32)
    for u in range(total // columns):
        span = slice(u * columns, (u + 1) * columns)
        value = keep_ref[0, :, span] + recv_ref[0, :, span]
        top = jnp.maximum(jnp.max(jnp.abs(value), axis=1, keepdims=True), 2.0**-100)
        power = jnp.ceil(jnp.log2(top)) - 15.0
        scaled = jnp.clip(jnp.round(value * jnp.exp2(-power)), -32767.0, 32767.0)
        out_ref[0, :, at + u * columns : at + (u + 1) * columns] = scaled.astype(jnp.int32).astype(jnp.int16)
        exponents = jnp.where(lane == at // columns + u, power.astype(jnp.int32), exponents)
    out_ref[0, :, at + total :] = exponents.astype(jnp.int16)


def pack(keep, recv, before=()):
    n, width, total = keep.shape
    columns = total + (before[0].shape[2] if before else 128)

    def spec(v):
        return pl.BlockSpec((1,) + v.shape[1:], lambda t: (t, 0, 0))

    out = jax.ShapeDtypeStruct((n, width, columns), jnp.int16)
    return pl.pallas_call(
        pack_kernel,
        out_shape=out,
        grid=(n,),
        in_specs=[spec(v) for v in (keep, recv, *before)],
        out_specs=spec(out),
        compiler_params=pltpu.CompilerParams(vmem_limit_bytes=8 * 2**20),
        cost_estimate=CHEAP,
    )(keep, recv, *before)


def products_kernel(plan, n_f, n_g, at_ref, *refs):
    f_refs, g_refs = refs[:n_f], refs[n_f : n_f + n_g]
    away_ref, keep_ref, joined = refs[n_f + n_g :]
    columns = g_refs[0].shape[1]
    first_core = at_ref[0] == 0
    for j, ref in enumerate(g_refs):
        joined[:, j * columns : (j + 1) * columns] = ref[...]
    at = 0
    for pieces, lo, hi in plan:
        span = (hi - lo) * columns
        parts = []
        for i, part in pieces:
            n, cores, width, depth = f_refs[i].shape
            value = f_refs[i][...] if part is None else f_refs[i][part * (n // 2) : (part + 1) * (n // 2)]
            parts.append(value.reshape(-1, depth))
        lhs = parts[0] if len(parts) == 1 else jnp.concatenate(parts, axis=0)
        out = jnp.dot(lhs, joined[:, lo * columns : hi * columns], preferred_element_type=jnp.float32)
        out = out.reshape(NX, NC, width, span)
        keep_ref[:, :, at : at + span] = jnp.where(first_core, out[:, 0], out[:, 1])
        away_ref[:, :, at : at + span] = jnp.where(first_core, out[:, 1], out[:, 0])
        at += span


def products(plan, at, f_arrays, g_pieces):
    width, rows = f_arrays[0].shape[2:]
    columns = g_pieces[0].shape[1]
    units = sum(hi - lo for _, lo, hi in plan)
    terms = jax.ShapeDtypeStruct((NX, width, units * columns), jnp.float32)
    return pl.pallas_call(
        functools.partial(products_kernel, plan, len(f_arrays), len(g_pieces)),
        out_shape=[terms, terms],
        in_specs=[SMEM] + [VMEM] * (len(f_arrays) + len(g_pieces)),
        out_specs=[VMEM] * 2,
        scratch_shapes=[pltpu.VMEM((rows, len(g_pieces) * columns), jnp.bfloat16)],
        compiler_params=pltpu.CompilerParams(vmem_limit_bytes=26 * 2**20),
        cost_estimate=CHEAP,
    )(at, *f_arrays, *g_pieces)


def facts_kernel(normalizer, at_ref, pair_ref, block_ref, live_ref, weight_ref, mask_ref):
    columns = mask_ref.shape[1] // NZ
    lane = lax.broadcasted_iota(jnp.int32, (1, weight_ref.shape[1]), 1)
    z, y = at_ref[1], at_ref[2]
    own = [lax.rem(z + e, NZ) * NY + y for e in range(NZ)]
    own = [own[e] for e in ORDER]
    for i, slot in enumerate(own):
        live = jnp.full((1, columns), live_ref[slot].astype(jnp.float32))
        mask_ref[:, i * columns : (i + 1) * columns] = live
    for k in range(NY - 1):
        for i, f in enumerate(ORDER):
            other = lax.rem(z + f, NZ) * NY + lax.rem(y + k, NY)
            for j, slot in enumerate(own):
                alike = (block_ref[other] == block_ref[slot]).astype(jnp.int32)
                value = (alike * live_ref[other] * live_ref[slot]).astype(jnp.float32) * normalizer
                row = jnp.where(lane == 2 * pair_ref[other] + pair_ref[slot], value, 0.0)
                if k == 1:
                    row = row + jnp.where(lane == 2 * pair_ref[slot] + pair_ref[other], value, 0.0)
                n = (k * NZ + i) * NZ + j
                weight_ref[n : n + 1] = row


def facts(at, pair, block, live, normalizer, columns):
    return pl.pallas_call(
        functools.partial(facts_kernel, normalizer),
        out_shape=[
            jax.ShapeDtypeStruct(((NY - 1) * NZ * NZ, 128), jnp.float32),
            jax.ShapeDtypeStruct((1, NZ * columns), jnp.float32),
        ],
        in_specs=[SMEM] * 4,
        out_specs=[VMEM] * 2,
        compiler_params=pltpu.CompilerParams(vmem_limit_bytes=4 * 2**20),
        cost_estimate=CHEAP,
    )(at, pair, block, live)


def finish_kernel(plan, n_rows, at_ref, total_ref, mask_ref, weight_ref, *refs):
    row_refs, done_refs = refs[:n_rows], refs[n_rows : n_rows + NY]
    bmat_ref, held, arrived, dots = refs[n_rows + NY :]
    n, width, _ = held.shape
    columns = dots.shape[1]
    copies = [pltpu.make_async_copy(total_ref.at[t], held.at[t], arrived.at[t]) for t in range(n)]
    for copy in copies:
        copy.start()
    for copy in copies:
        copy.wait()
    units = held.shape[2] - columns
    scales = [jnp.exp2(held[t, :, units:].astype(jnp.int32).astype(jnp.float32)) for t in range(n)]
    u = 0
    for j, es in plan:
        for e in es:
            value = 0.0
            for t in range(n):
                term = held[t, :, u * columns : (u + 1) * columns].astype(jnp.int32).astype(jnp.float32)
                value = value + term * scales[t][:, u : u + 1]
            value = value * mask_ref[:, e * columns : (e + 1) * columns]
            done_refs[j][:, e * columns : (e + 1) * columns] = value.astype(jnp.bfloat16)
            u += 1
    starts = [pl.multiple_of(lax.rem(at_ref[2] + offset_at(j, at_ref[3]), NY) * width, 16) for j in range(NY)]
    for k in range(n_rows):
        for f in range(NZ):
            sums = [0.0] * NZ
            for start, done_ref in zip(starts, done_refs):
                row = row_refs[k][pl.ds(start, width), f * columns : (f + 1) * columns].astype(jnp.float32)
                for e in range(NZ):
                    term = row * done_ref[:, e * columns : (e + 1) * columns].astype(jnp.float32)
                    sums[e] = sums[e] + term.reshape(width // 8, 8, columns).sum(0)
            for e in range(NZ):
                i = (k * NZ + f) * NZ + e
                dots[i : i + 1] = sums[e].sum(0, keepdims=True)
    bmat_ref[...] = (dots[...].sum(1, keepdims=True) * weight_ref[...]).sum(0, keepdims=True)


def finish(plan, at, total, mask, weight, rows):
    columns = rows[0].shape[1] // NZ
    done = jax.ShapeDtypeStruct((total.shape[1], NZ * columns), jnp.bfloat16)
    return pl.pallas_call(
        functools.partial(finish_kernel, plan, len(rows)),
        out_shape=[done] * NY + [jax.ShapeDtypeStruct((1, weight.shape[1]), jnp.float32)],
        in_specs=[SMEM, ANY] + [VMEM] * (2 + len(rows)),
        out_specs=[VMEM] * (NY + 1),
        scratch_shapes=[
            pltpu.VMEM(total.shape, total.dtype),
            pltpu.SemaphoreType.DMA((total.shape[0],)),
            pltpu.VMEM((weight.shape[0], columns), jnp.float32),
        ],
        compiler_params=pltpu.CompilerParams(vmem_limit_bytes=16 * 2**20),
        cost_estimate=CHEAP,
    )(at, total, mask, weight, *rows)


def rows_kernel(n, at_ref, *refs):
    g_refs, (out_ref, arrived) = refs[:n], refs[n:]
    count, columns = out_ref.shape[0], g_refs[0].shape[1]
    start = pl.multiple_of(at_ref[1] * count, 64)
    copies = [
        pltpu.make_async_copy(
            ref.at[pl.ds(start, count)], out_ref.at[:, j * columns : (j + 1) * columns], arrived.at[j]
        )
        for j, ref in enumerate(g_refs)
    ]
    for copy in copies:
        copy.start()
    for copy in copies:
        copy.wait()


def rows_of(at, g, count):
    return pl.pallas_call(
        functools.partial(rows_kernel, len(g)),
        out_shape=jax.ShapeDtypeStruct((count, len(g) * g[0].shape[1]), g[0].dtype),
        in_specs=[SMEM] + [ANY] * len(g),
        out_specs=VMEM,
        scratch_shapes=[pltpu.SemaphoreType.DMA((len(g),))],
        compiler_params=pltpu.CompilerParams(vmem_limit_bytes=4 * 2**20),
        cost_estimate=CHEAP,
    )(at, *g)


def place_kernel(at_ref, *refs):
    *piece_refs, out_ref = refs
    columns = out_ref.shape[2]
    for k, piece_ref in enumerate(piece_refs):
        owner = lax.rem(at_ref[2] + NY - offset_at(k, at_ref[3]), NY)
        for j, e in enumerate(ORDER):
            slot = lax.rem(at_ref[1] + e, NZ) * NY + owner
            out_ref[slot] = piece_ref[:, j * columns : (j + 1) * columns]


def place(at, pieces, columns):
    width = pieces[0].shape[0]
    return pl.pallas_call(
        place_kernel,
        out_shape=jax.ShapeDtypeStruct((NZ * NY, width, columns), jnp.bfloat16),
        in_specs=[SMEM] + [VMEM] * len(pieces),
        out_specs=VMEM,
        compiler_params=pltpu.CompilerParams(vmem_limit_bytes=8 * 2**20),
        cost_estimate=CHEAP,
    )(at, *pieces)


def on_device(geminal, fock_matrix, slot_occupied_pair, slot_column_block, slot_live):
    n_fock, _, width, panel_rows = fock_matrix.shape
    columns = geminal.shape[2]
    n_slots = NZ * NY
    z, y, x = lax.axis_index("z"), lax.axis_index("y"), lax.axis_index("x")
    at = jnp.stack([lax.axis_index("c"), z, y, x])
    normalizer = 1.0 / (panel_rows * n_fock * columns)

    own = fock_matrix.reshape(NX, NC, width, panel_rows)
    low, high = split(own)
    g, low, high = lax.optimization_barrier((geminal[0], low, high))
    from_left, from_right = shift_y(low, 1), shift_y(high, -1)
    to_right, to_left = join(low, high, from_left, from_right)
    after_left, after_right = shift_y(to_right, 1), shift_y(to_left, -1)
    f_arrays = [own, from_left, from_right, after_left, after_right]
    f_blocks = (((0, None),), ((1, None), (2, None)), ((4, 0), (3, 1)), ((3, 0), (4, 1)))

    slots = {0: g}
    slots[1], slots[7] = shift_z(slots[0], -1), shift_z(slots[0], 1)
    slots[2], slots[6] = shift_z(slots[1], -1), shift_z(slots[7], 1)
    slots[3], slots[5] = shift_z(slots[2], -1), shift_z(slots[6], 1)

    weight, mask = facts(at, slot_occupied_pair, slot_column_block, slot_live, normalizer, columns)

    def start(plan, order, arrays):
        plan = tuple((f_blocks[j], order.index(es[0]), order.index(es[0]) + len(es)) for j, es in plan)
        away, keep = products(plan, at, arrays, [slots[e] for e in order])
        return swap_core(away), keep

    def spread(total):
        return lax.all_to_all(total, "x", 0, 0)

    def places(plan):
        return tuple((j, tuple(ORDER.index(e) for e in es)) for j, es in plan)

    first = lax.optimization_barrier((*f_arrays[:3], to_right, to_left))[:3]
    recv, keep = start(FIRST, NEAR, list(first))
    packed = pack(keep, recv)
    slots[4] = shift_z(slots[5], 1)

    rows = [rows_of(at, [slots[e] for e in ORDER], NY * width)]
    rows.append(shift_y(rows[0], -1))
    rows.append(shift_y(rows[1], -1))

    recv, keep = start(SECOND, ORDER, f_arrays)
    total = spread(pack(keep, recv, (packed,)))
    *done, bmat = finish(places(FIRST + SECOND), at, total, mask, weight, rows)
    bmat = total_over(bmat, "z", NZ)
    pieces = [to_owner(v, j) for j, v in enumerate(done)]
    *pieces, bmat = lax.optimization_barrier((*pieces, bmat))

    out = place(at, pieces, columns)
    return out, total_over(bmat, ("y", "x", "c"), NY * NX * NC)[0, :4].reshape(2, 2)


def solution(mesh):
    mesh = Mesh(mesh.devices.reshape(NZ, NY, NX, NC), ("z", "y", "x", "c"))
    pair, fock = ("z", "y"), ("x", "c")
    return jax.shard_map(
        on_device,
        mesh=mesh,
        in_specs=(P(pair, fock, None), P(None, pair, None, fock), P(), P(), P()),
        out_specs=(P(None, fock + pair, None), P()),
        check_vma=False,
    )
```

```python
import functools

import jax
import jax.numpy as jnp
from jax import lax
from jax.experimental import pallas as pl
from jax.experimental.pallas import tpu as pltpu
from jax.sharding import Mesh
from jax.sharding import PartitionSpec as P

HIGHEST = lax.Precision.HIGHEST
NZ, NY, NX, NC = 8, 4, 4, 2
VMEM = pl.BlockSpec(memory_space=pltpu.VMEM)
SMEM = pl.BlockSpec(memory_space=pltpu.SMEM)
ANY = pl.BlockSpec(memory_space=pl.ANY)
TAIL = 16
CHEAP = pl.CostEstimate(flops=1, bytes_accessed=1, transcendentals=0)

NEAR, FAR = (0, 1, 7, 2, 6), (3, 5, 4)
ORDER = NEAR + FAR
FIRST = ((0, NEAR), (1, NEAR))
SECOND = ((0, FAR), (1, FAR), (2, ORDER), (3, ORDER))


def offset(j, x):
    return (0, -1, 1, 2)[j] if x < NX // 2 else (0, 1, -1, 2)[j]


def offset_at(j, x):
    near, far = jnp.where(x < NX // 2, NY - 1, 1), jnp.where(x < NX // 2, 1, NY - 1)
    return (0, near, far, 2)[j]


def shift_z(v, s):
    return lax.ppermute(v, "z", [(z, (z + s) % NZ) for z in range(NZ)])


def shift_y(v, s):
    return lax.ppermute(v, "y", [(y, (y + s) % NY) for y in range(NY)])


def to_owner(v, j):
    moves = []
    for y in range(NY):
        for x in range(NX):
            moves.append((y * NX + x, (y + offset(j, x)) % NY * NX + x))
    return lax.ppermute(v, ("y", "x"), moves) if j else v


def swap_core(v):
    return lax.ppermute(v, "c", [(0, 1), (1, 0)])


def split_kernel(own_ref, low_ref, high_ref):
    half = own_ref.shape[0] // 2
    low_ref[...] = own_ref[:half]
    high_ref[...] = own_ref[half:]


def split(own):
    half = jax.ShapeDtypeStruct((own.shape[0] // 2,) + own.shape[1:], own.dtype)
    return pl.pallas_call(
        split_kernel,
        out_shape=[half, half],
        in_specs=[VMEM],
        out_specs=[VMEM] * 2,
        compiler_params=pltpu.CompilerParams(vmem_limit_bytes=8 * 2**20),
        cost_estimate=CHEAP,
    )(own)


def join_kernel(low_ref, high_ref, left_ref, right_ref, to_right_ref, to_left_ref):
    half = low_ref.shape[0]
    to_right_ref[:half] = left_ref[...]
    to_right_ref[half:] = high_ref[...]
    to_left_ref[:half] = low_ref[...]
    to_left_ref[half:] = right_ref[...]


def join(low, high, left, right):
    whole = jax.ShapeDtypeStruct((2 * low.shape[0],) + low.shape[1:], low.dtype)
    return pl.pallas_call(
        join_kernel,
        out_shape=[whole, whole],
        in_specs=[VMEM] * 4,
        out_specs=[VMEM] * 2,
        compiler_params=pltpu.CompilerParams(vmem_limit_bytes=12 * 2**20),
        cost_estimate=CHEAP,
    )(low, high, left, right)


def pack_kernel(keep_ref, recv_ref, *refs):
    *before_ref, out_ref = refs
    _, width, total = keep_ref.shape
    columns = 128
    lane = lax.broadcasted_iota(jnp.int32, (width, columns), 1)
    at = 0
    exponents = jnp.zeros((width, columns), jnp.int32)
    for ref in before_ref:
        at = ref.shape[2] - columns
        out_ref[0, :, :at] = ref[0, :, :at]
        exponents = ref[0, :, at:].astype(jnp.int32)
    for u in range(total // columns):
        span = slice(u * columns, (u + 1) * columns)
        value = keep_ref[0, :, span] + recv_ref[0, :, span]
        top = jnp.maximum(jnp.max(jnp.abs(value), axis=1, keepdims=True), 2.0**-100)
        power = jnp.ceil(jnp.log2(top)) - 15.0
        scaled = jnp.clip(jnp.round(value * jnp.exp2(-power)), -32767.0, 32767.0)
        out_ref[0, :, at + u * columns : at + (u + 1) * columns] = scaled.astype(jnp.int32).astype(jnp.int16)
        exponents = jnp.where(lane == at // columns + u, power.astype(jnp.int32), exponents)
    out_ref[0, :, at + total :] = exponents.astype(jnp.int16)


def pack(keep, recv, before=()):
    n, width, total = keep.shape
    columns = total + (before[0].shape[2] if before else 128)

    def spec(v):
        return pl.BlockSpec((1,) + v.shape[1:], lambda t: (t, 0, 0))

    out = jax.ShapeDtypeStruct((n, width, columns), jnp.int16)
    return pl.pallas_call(
        pack_kernel,
        out_shape=out,
        grid=(n,),
        in_specs=[spec(v) for v in (keep, recv, *before)],
        out_specs=spec(out),
        compiler_params=pltpu.CompilerParams(vmem_limit_bytes=8 * 2**20),
        cost_estimate=CHEAP,
    )(keep, recv, *before)


def products_kernel(plan, n_f, n_g, at_ref, *refs):
    f_refs, g_refs = refs[:n_f], refs[n_f : n_f + n_g]
    away_ref, keep_ref, joined = refs[n_f + n_g :]
    columns = g_refs[0].shape[1]
    first_core = at_ref[0] == 0
    for j, ref in enumerate(g_refs):
        joined[:, j * columns : (j + 1) * columns] = ref[...]
    at = 0
    for pieces, lo, hi in plan:
        span = (hi - lo) * columns
        parts = []
        for i, part in pieces:
            n, cores, width, depth = f_refs[i].shape
            value = f_refs[i][...] if part is None else f_refs[i][part * (n // 2) : (part + 1) * (n // 2)]
            parts.append(value.reshape(-1, depth))
        lhs = parts[0] if len(parts) == 1 else jnp.concatenate(parts, axis=0)
        out = jnp.dot(lhs, joined[:, lo * columns : hi * columns], preferred_element_type=jnp.float32)
        out = out.reshape(NX, NC, width, span)
        keep_ref[:, :, at : at + span] = jnp.where(first_core, out[:, 0], out[:, 1])
        away_ref[:, :, at : at + span] = jnp.where(first_core, out[:, 1], out[:, 0])
        at += span


def products(plan, at, f_arrays, g_pieces):
    width, rows = f_arrays[0].shape[2:]
    columns = g_pieces[0].shape[1]
    units = sum(hi - lo for _, lo, hi in plan)
    terms = jax.ShapeDtypeStruct((NX, width, units * columns), jnp.float32)
    return pl.pallas_call(
        functools.partial(products_kernel, plan, len(f_arrays), len(g_pieces)),
        out_shape=[terms, terms],
        in_specs=[SMEM] + [VMEM] * (len(f_arrays) + len(g_pieces)),
        out_specs=[VMEM] * 2,
        scratch_shapes=[pltpu.VMEM((rows, len(g_pieces) * columns), jnp.bfloat16)],
        compiler_params=pltpu.CompilerParams(vmem_limit_bytes=26 * 2**20),
        cost_estimate=CHEAP,
    )(at, *f_arrays, *g_pieces)


def facts_kernel(normalizer, at_ref, pair_ref, block_ref, live_ref, weight_ref, mask_ref):
    columns = mask_ref.shape[1] // NZ
    lane = lax.broadcasted_iota(jnp.int32, (1, weight_ref.shape[1]), 1)
    z, y = at_ref[1], at_ref[2]
    own = [lax.rem(z + e, NZ) * NY + y for e in range(NZ)]
    own = [own[e] for e in ORDER]
    for i, slot in enumerate(own):
        live = jnp.full((1, columns), live_ref[slot].astype(jnp.float32))
        mask_ref[:, i * columns : (i + 1) * columns] = live
    for k in range(NY - 1):
        for i, f in enumerate(ORDER):
            other = lax.rem(z + f, NZ) * NY + lax.rem(y + k, NY)
            for j, slot in enumerate(own):
                alike = (block_ref[other] == block_ref[slot]).astype(jnp.int32)
                value = (alike * live_ref[other] * live_ref[slot]).astype(jnp.float32) * normalizer
                row = jnp.where(lane == 2 * pair_ref[other] + pair_ref[slot], value, 0.0)
                if k == 1:
                    row = row + jnp.where(lane == 2 * pair_ref[slot] + pair_ref[other], value, 0.0)
                n = (k * NZ + i) * NZ + j
                weight_ref[n : n + 1] = row


def facts(at, pair, block, live, normalizer, columns):
    return pl.pallas_call(
        functools.partial(facts_kernel, normalizer),
        out_shape=[
            jax.ShapeDtypeStruct(((NY - 1) * NZ * NZ, 128), jnp.float32),
            jax.ShapeDtypeStruct((1, NZ * columns), jnp.float32),
        ],
        in_specs=[SMEM] * 4,
        out_specs=[VMEM] * 2,
        compiler_params=pltpu.CompilerParams(vmem_limit_bytes=4 * 2**20),
        cost_estimate=CHEAP,
    )(at, pair, block, live)


def finish_kernel(plan, n_rows, at_ref, total_ref, mask_ref, weight_ref, *refs):
    row_refs, done_refs = refs[:n_rows], refs[n_rows : n_rows + NY]
    held, arrived, dots, made = refs[n_rows + NY :]
    n, width, _ = held.shape
    columns = dots.shape[1]
    copies = [pltpu.make_async_copy(total_ref.at[t], held.at[t], arrived.at[t]) for t in range(n)]
    for copy in copies:
        copy.start()
    for copy in copies:
        copy.wait()
    units = held.shape[2] - columns
    scales = [jnp.exp2(held[t, :, units:].astype(jnp.int32).astype(jnp.float32)) for t in range(n)]
    u = 0
    for j, es in plan:
        for e in es:
            value = 0.0
            for t in range(n):
                term = held[t, :, u * columns : (u + 1) * columns].astype(jnp.int32).astype(jnp.float32)
                value = value + term * scales[t][:, u : u + 1]
            value = value * mask_ref[:, e * columns : (e + 1) * columns]
            value = value.astype(jnp.bfloat16)
            done_refs[j][:width, e * columns : (e + 1) * columns] = value
            made[j, :, e * columns : (e + 1) * columns] = value.astype(jnp.float32)
            u += 1
    starts = [pl.multiple_of(lax.rem(at_ref[2] + offset_at(j, at_ref[3]), NY) * width, 16) for j in range(NY)]
    for k in range(n_rows):
        for f in range(NZ):
            sums = [0.0] * NZ
            for j, start in enumerate(starts):
                row = row_refs[k][pl.ds(start, width), f * columns : (f + 1) * columns].astype(jnp.float32)
                for e in range(NZ):
                    term = row * made[j, :, e * columns : (e + 1) * columns]
                    sums[e] = sums[e] + term.reshape(width // 8, 8, columns).sum(0)
            for e in range(NZ):
                i = (k * NZ + f) * NZ + e
                dots[i : i + 1] = sums[e].sum(0, keepdims=True)
    bmat = (dots[...].sum(1, keepdims=True) * weight_ref[...]).sum(0, keepdims=True)
    row = lax.broadcasted_iota(jnp.int32, (TAIL, columns), 0)
    tail = jnp.zeros((TAIL, columns), jnp.float32)
    for i in range(3):
        part = bmat.astype(jnp.bfloat16).astype(jnp.float32)
        tail = jnp.where(row == i, part, tail)
        bmat = bmat - part
    for done_ref in done_refs:
        done_ref[width:, :columns] = tail.astype(jnp.bfloat16)
        done_ref[width:, columns:] = jnp.zeros((TAIL, (NZ - 1) * columns), jnp.bfloat16)


def finish(plan, at, total, mask, weight, rows):
    columns = rows[0].shape[1] // NZ
    done = jax.ShapeDtypeStruct((total.shape[1] + TAIL, NZ * columns), jnp.bfloat16)
    return pl.pallas_call(
        functools.partial(finish_kernel, plan, len(rows)),
        out_shape=[done] * NY,
        in_specs=[SMEM, ANY] + [VMEM] * (2 + len(rows)),
        out_specs=[VMEM] * NY,
        scratch_shapes=[
            pltpu.VMEM(total.shape, total.dtype),
            pltpu.SemaphoreType.DMA((total.shape[0],)),
            pltpu.VMEM((weight.shape[0], columns), jnp.float32),
            pltpu.VMEM((NY, total.shape[1], NZ * columns), jnp.float32),
        ],
        compiler_params=pltpu.CompilerParams(vmem_limit_bytes=16 * 2**20),
        cost_estimate=CHEAP,
    )(at, total, mask, weight, *rows)


def rows_kernel(n, at_ref, *refs):
    g_refs, (out_ref, arrived) = refs[:n], refs[n:]
    count, columns = out_ref.shape[0], g_refs[0].shape[1]
    start = pl.multiple_of(at_ref[1] * count, 64)
    copies = [
        pltpu.make_async_copy(
            ref.at[pl.ds(start, count)], out_ref.at[:, j * columns : (j + 1) * columns], arrived.at[j]
        )
        for j, ref in enumerate(g_refs)
    ]
    for copy in copies:
        copy.start()
    for copy in copies:
        copy.wait()


def rows_of(at, g, count):
    return pl.pallas_call(
        functools.partial(rows_kernel, len(g)),
        out_shape=jax.ShapeDtypeStruct((count, len(g) * g[0].shape[1]), g[0].dtype),
        in_specs=[SMEM] + [ANY] * len(g),
        out_specs=VMEM,
        scratch_shapes=[pltpu.SemaphoreType.DMA((len(g),))],
        compiler_params=pltpu.CompilerParams(vmem_limit_bytes=4 * 2**20),
        cost_estimate=CHEAP,
    )(at, *g)


def place_kernel(at_ref, *refs):
    *piece_refs, out_ref, bmat_ref = refs
    _, width, columns = out_ref.shape
    bmat = 0.0
    for k, piece_ref in enumerate(piece_refs):
        owner = lax.rem(at_ref[2] + NY - offset_at(k, at_ref[3]), NY)
        for j, e in enumerate(ORDER):
            slot = lax.rem(at_ref[1] + e, NZ) * NY + owner
            out_ref[slot] = piece_ref[:width, j * columns : (j + 1) * columns]
        tail = piece_ref[width:, :columns].astype(jnp.float32)
        bmat = bmat + tail.sum(0, keepdims=True)
    bmat_ref[...] = jnp.broadcast_to(bmat, bmat_ref.shape)


def place(at, pieces, columns):
    width = pieces[0].shape[0] - TAIL
    return pl.pallas_call(
        place_kernel,
        out_shape=[
            jax.ShapeDtypeStruct((NZ * NY, width, columns), jnp.bfloat16),
            jax.ShapeDtypeStruct((NZ * NX * NC, columns), jnp.float32),
        ],
        in_specs=[SMEM] + [VMEM] * len(pieces),
        out_specs=[VMEM] * 2,
        compiler_params=pltpu.CompilerParams(vmem_limit_bytes=8 * 2**20),
        cost_estimate=CHEAP,
    )(at, *pieces)


def on_device(geminal, fock_matrix, slot_occupied_pair, slot_column_block, slot_live):
    n_fock, _, width, panel_rows = fock_matrix.shape
    columns = geminal.shape[2]
    n_slots = NZ * NY
    z, y, x = lax.axis_index("z"), lax.axis_index("y"), lax.axis_index("x")
    at = jnp.stack([lax.axis_index("c"), z, y, x])
    normalizer = 1.0 / (panel_rows * n_fock * columns)

    own = fock_matrix.reshape(NX, NC, width, panel_rows)
    low, high = split(own)
    g, low, high = lax.optimization_barrier((geminal[0], low, high))
    from_left, from_right = shift_y(low, 1), shift_y(high, -1)
    to_right, to_left = join(low, high, from_left, from_right)
    after_left, after_right = shift_y(to_right, 1), shift_y(to_left, -1)
    f_arrays = [own, from_left, from_right, after_left, after_right]
    f_blocks = (((0, None),), ((1, None), (2, None)), ((4, 0), (3, 1)), ((3, 0), (4, 1)))

    slots = {0: g}
    slots[1], slots[7] = shift_z(slots[0], -1), shift_z(slots[0], 1)
    slots[2], slots[6] = shift_z(slots[1], -1), shift_z(slots[7], 1)
    slots[3], slots[5] = shift_z(slots[2], -1), shift_z(slots[6], 1)

    weight, mask = facts(at, slot_occupied_pair, slot_column_block, slot_live, normalizer, columns)

    def start(plan, order, arrays):
        plan = tuple((f_blocks[j], order.index(es[0]), order.index(es[0]) + len(es)) for j, es in plan)
        away, keep = products(plan, at, arrays, [slots[e] for e in order])
        return swap_core(away), keep

    def spread(total):
        return lax.all_to_all(total, "x", 0, 0)

    def places(plan):
        return tuple((j, tuple(ORDER.index(e) for e in es)) for j, es in plan)

    first = lax.optimization_barrier((*f_arrays[:3], to_right, to_left))[:3]
    recv, keep = start(FIRST, NEAR, list(first))
    packed = pack(keep, recv)
    slots[4] = shift_z(slots[5], 1)

    rows = [rows_of(at, [slots[e] for e in ORDER], NY * width)]
    rows.append(shift_y(rows[0], -1))
    rows.append(shift_y(rows[1], -1))

    rows[0], *f_arrays = lax.optimization_barrier((rows[0], *f_arrays))
    recv, keep = start(SECOND, ORDER, f_arrays)
    total = spread(pack(keep, recv, (packed,)))
    done = finish(places(FIRST + SECOND), at, total, mask, weight, rows)
    out, bmat = place(at, [to_owner(v, j) for j, v in enumerate(done)], columns)
    bmat = lax.all_to_all(bmat, ("z", "x", "c"), 0, 0, tiled=True)
    return out, bmat[:, :4].sum(0).reshape(2, 2)


def solution(mesh):
    mesh = Mesh(mesh.devices.reshape(NZ, NY, NX, NC), ("z", "y", "x", "c"))
    pair, fock = ("z", "y"), ("x", "c")
    return jax.shard_map(
        on_device,
        mesh=mesh,
        in_specs=(P(pair, fock, None), P(None, pair, None, fock), P(), P(), P()),
        out_specs=(P(None, fock + pair, None), P()),
        check_vma=False,
    )
```

```python
import functools

import jax
import jax.numpy as jnp
from jax import lax
from jax.experimental import pallas as pl
from jax.experimental.pallas import tpu as pltpu
from jax.sharding import Mesh
from jax.sharding import PartitionSpec as P

HIGHEST = lax.Precision.HIGHEST
NZ, NY, NX, NC = 8, 4, 4, 2
VMEM = pl.BlockSpec(memory_space=pltpu.VMEM)
SMEM = pl.BlockSpec(memory_space=pltpu.SMEM)
ANY = pl.BlockSpec(memory_space=pl.ANY)
TAIL = 16
CHEAP = pl.CostEstimate(flops=1, bytes_accessed=1, transcendentals=0)

NEAR, FAR = (0, 1, 7, 2, 6), (3, 5, 4)
ORDER = NEAR + FAR
FIRST = ((0, NEAR), (1, NEAR))
SECOND = ((0, FAR), (1, FAR), (2, ORDER), (3, ORDER))


def offset(j, x):
    return (0, -1, 1, 2)[j] if x < NX // 2 else (0, 1, -1, 2)[j]


def offset_at(j, x):
    near, far = jnp.where(x < NX // 2, NY - 1, 1), jnp.where(x < NX // 2, 1, NY - 1)
    return (0, near, far, 2)[j]


def shift_z(v, s):
    return lax.ppermute(v, "z", [(z, (z + s) % NZ) for z in range(NZ)])


def shift_y(v, s):
    return lax.ppermute(v, "y", [(y, (y + s) % NY) for y in range(NY)])


def to_owner(v, j):
    moves = []
    for y in range(NY):
        for x in range(NX):
            moves.append((y * NX + x, (y + offset(j, x)) % NY * NX + x))
    return lax.ppermute(v, ("y", "x"), moves) if j else v


def swap_core(v):
    return lax.ppermute(v, "c", [(0, 1), (1, 0)])


def split_kernel(own_ref, low_ref, high_ref):
    half = own_ref.shape[0] // 2
    low_ref[...] = own_ref[:half]
    high_ref[...] = own_ref[half:]


def split(own):
    half = jax.ShapeDtypeStruct((own.shape[0] // 2,) + own.shape[1:], own.dtype)
    return pl.pallas_call(
        split_kernel,
        out_shape=[half, half],
        in_specs=[VMEM],
        out_specs=[VMEM] * 2,
        compiler_params=pltpu.CompilerParams(vmem_limit_bytes=8 * 2**20),
        cost_estimate=CHEAP,
    )(own)


def join_kernel(low_ref, high_ref, left_ref, right_ref, to_right_ref, to_left_ref, arrived):
    half = low_ref.shape[0]
    moves = [
        (left_ref, to_right_ref.at[:half]),
        (right_ref, to_left_ref.at[half:]),
        (high_ref, to_right_ref.at[half:]),
        (low_ref, to_left_ref.at[:half]),
    ]
    copies = [pltpu.make_async_copy(a, b, arrived.at[i]) for i, (a, b) in enumerate(moves)]
    for copy in copies:
        copy.start()
    for copy in copies:
        copy.wait()


def join(low, high, left, right):
    whole = jax.ShapeDtypeStruct((2 * low.shape[0],) + low.shape[1:], low.dtype)
    return pl.pallas_call(
        join_kernel,
        out_shape=[whole, whole],
        in_specs=[ANY] * 4,
        out_specs=[ANY] * 2,
        scratch_shapes=[pltpu.SemaphoreType.DMA((4,))],
        compiler_params=pltpu.CompilerParams(vmem_limit_bytes=4 * 2**20),
        cost_estimate=CHEAP,
    )(low, high, left, right)


def pack_kernel(keep_ref, recv_ref, *refs):
    *before_ref, out_ref = refs
    _, width, total = keep_ref.shape
    columns = 128
    lane = lax.broadcasted_iota(jnp.int32, (width, columns), 1)
    at = 0
    exponents = jnp.zeros((width, columns), jnp.int32)
    for ref in before_ref:
        at = ref.shape[2] - columns
        out_ref[0, :, :at] = ref[0, :, :at]
        exponents = ref[0, :, at:].astype(jnp.int32)
    for u in range(total // columns):
        span = slice(u * columns, (u + 1) * columns)
        value = keep_ref[0, :, span] + recv_ref[0, :, span]
        top = jnp.maximum(jnp.max(jnp.abs(value), axis=1, keepdims=True), 2.0**-110)
        power = jnp.ceil(jnp.log2(top)) - 15.0
        scaled = jnp.clip(jnp.round(value * jnp.exp2(-power)), -32767.0, 32767.0)
        out_ref[0, :, at + u * columns : at + (u + 1) * columns] = scaled.astype(jnp.int32).astype(jnp.int16)
        exponents = jnp.where(lane == at // columns + u, power.astype(jnp.int32), exponents)
    out_ref[0, :, at + total :] = exponents.astype(jnp.int16)


def pack(keep, recv, before=()):
    n, width, total = keep.shape
    columns = total + (before[0].shape[2] if before else 128)

    def spec(v):
        return pl.BlockSpec((1,) + v.shape[1:], lambda t: (t, 0, 0))

    out = jax.ShapeDtypeStruct((n, width, columns), jnp.int16)
    return pl.pallas_call(
        pack_kernel,
        out_shape=out,
        grid=(n,),
        in_specs=[spec(v) for v in (keep, recv, *before)],
        out_specs=spec(out),
        compiler_params=pltpu.CompilerParams(vmem_limit_bytes=8 * 2**20),
        cost_estimate=CHEAP,
    )(keep, recv, *before)


def products_kernel(plan, n_f, n_g, at_ref, *refs):
    f_refs, g_refs = refs[:n_f], refs[n_f : n_f + n_g]
    away_ref, keep_ref, joined = refs[n_f + n_g :]
    columns = g_refs[0].shape[1]
    first_core = at_ref[0] == 0
    for j, ref in enumerate(g_refs):
        joined[:, j * columns : (j + 1) * columns] = ref[...]
    at = 0
    for pieces, lo, hi in plan:
        span = (hi - lo) * columns
        parts = []
        for i, part in pieces:
            n, cores, width, depth = f_refs[i].shape
            value = f_refs[i][...] if part is None else f_refs[i][part * (n // 2) : (part + 1) * (n // 2)]
            parts.append(value.reshape(-1, depth))
        lhs = parts[0] if len(parts) == 1 else jnp.concatenate(parts, axis=0)
        out = jnp.dot(lhs, joined[:, lo * columns : hi * columns], preferred_element_type=jnp.float32)
        out = out.reshape(NX, NC, width, span)
        keep_ref[:, :, at : at + span] = jnp.where(first_core, out[:, 0], out[:, 1])
        away_ref[:, :, at : at + span] = jnp.where(first_core, out[:, 1], out[:, 0])
        at += span


def products(plan, at, f_arrays, g_pieces):
    width, rows = f_arrays[0].shape[2:]
    columns = g_pieces[0].shape[1]
    units = sum(hi - lo for _, lo, hi in plan)
    terms = jax.ShapeDtypeStruct((NX, width, units * columns), jnp.float32)
    return pl.pallas_call(
        functools.partial(products_kernel, plan, len(f_arrays), len(g_pieces)),
        out_shape=[terms, terms],
        in_specs=[SMEM] + [VMEM] * (len(f_arrays) + len(g_pieces)),
        out_specs=[VMEM] * 2,
        scratch_shapes=[pltpu.VMEM((rows, len(g_pieces) * columns), jnp.bfloat16)],
        compiler_params=pltpu.CompilerParams(vmem_limit_bytes=26 * 2**20),
        cost_estimate=CHEAP,
    )(at, *f_arrays, *g_pieces)


def facts_kernel(normalizer, at_ref, pair_ref, block_ref, live_ref, weight_ref, mask_ref):
    columns = mask_ref.shape[1] // NZ
    lane = lax.broadcasted_iota(jnp.int32, (1, weight_ref.shape[1]), 1)
    z, y = at_ref[1], at_ref[2]
    own = [lax.rem(z + e, NZ) * NY + y for e in range(NZ)]
    own = [own[e] for e in ORDER]
    for i, slot in enumerate(own):
        live = jnp.full((1, columns), live_ref[slot].astype(jnp.float32))
        mask_ref[:, i * columns : (i + 1) * columns] = live
    for k in range(NY - 1):
        for i, f in enumerate(ORDER):
            other = lax.rem(z + f, NZ) * NY + lax.rem(y + k, NY)
            for j, slot in enumerate(own):
                alike = (block_ref[other] == block_ref[slot]).astype(jnp.int32)
                value = (alike * live_ref[other] * live_ref[slot]).astype(jnp.float32) * normalizer
                row = jnp.where(lane == 2 * pair_ref[other] + pair_ref[slot], value, 0.0)
                if k == 1:
                    row = row + jnp.where(lane == 2 * pair_ref[slot] + pair_ref[other], value, 0.0)
                n = (k * NZ + i) * NZ + j
                weight_ref[n : n + 1] = row


def facts(at, pair, block, live, normalizer, columns):
    return pl.pallas_call(
        functools.partial(facts_kernel, normalizer),
        out_shape=[
            jax.ShapeDtypeStruct(((NY - 1) * NZ * NZ, 128), jnp.float32),
            jax.ShapeDtypeStruct((1, NZ * columns), jnp.float32),
        ],
        in_specs=[SMEM] * 4,
        out_specs=[VMEM] * 2,
        compiler_params=pltpu.CompilerParams(vmem_limit_bytes=4 * 2**20),
        cost_estimate=CHEAP,
    )(at, pair, block, live)


def finish_kernel(plan, n_rows, at_ref, total_ref, mask_ref, weight_ref, *refs):
    row_refs, done_refs = refs[:n_rows], refs[n_rows : n_rows + NY]
    dots, made = refs[n_rows + NY :]
    n, width, _ = total_ref.shape
    columns = dots.shape[1]
    units = total_ref.shape[2] - columns
    scales = [jnp.exp2(total_ref[t, :, units:].astype(jnp.int32).astype(jnp.float32)) for t in range(n)]
    u = 0
    for j, es in plan:
        for e in es:
            value = 0.0
            for t in range(n):
                term = total_ref[t, :, u * columns : (u + 1) * columns].astype(jnp.int32).astype(jnp.float32)
                value = value + term * scales[t][:, u : u + 1]
            value = value * mask_ref[:, e * columns : (e + 1) * columns]
            value = value.astype(jnp.bfloat16)
            done_refs[j][:width, e * columns : (e + 1) * columns] = value
            made[j, :, e * columns : (e + 1) * columns] = value.astype(jnp.float32)
            u += 1
    starts = [pl.multiple_of(lax.rem(at_ref[2] + offset_at(j, at_ref[3]), NY) * width, 16) for j in range(NY)]
    for k in range(n_rows):
        for f in range(NZ):
            sums = [0.0] * NZ
            for j, start in enumerate(starts):
                row = row_refs[k][pl.ds(start, width), f * columns : (f + 1) * columns].astype(jnp.float32)
                for e in range(NZ):
                    term = row * made[j, :, e * columns : (e + 1) * columns]
                    sums[e] = sums[e] + term.reshape(width // 8, 8, columns).sum(0)
            for e in range(NZ):
                i = (k * NZ + f) * NZ + e
                dots[i : i + 1] = sums[e].sum(0, keepdims=True)
    bmat = (dots[...].sum(1, keepdims=True) * weight_ref[...]).sum(0, keepdims=True)
    row = lax.broadcasted_iota(jnp.int32, (TAIL, columns), 0)
    tail = jnp.zeros((TAIL, columns), jnp.float32)
    for i in range(3):
        part = bmat.astype(jnp.bfloat16).astype(jnp.float32)
        tail = jnp.where(row == i, part, tail)
        bmat = bmat - part
    for done_ref in done_refs:
        done_ref[width:, :columns] = tail.astype(jnp.bfloat16)
        done_ref[width:, columns:] = jnp.zeros((TAIL, (NZ - 1) * columns), jnp.bfloat16)


def finish(plan, at, total, mask, weight, rows):
    columns = rows[0].shape[1] // NZ
    done = jax.ShapeDtypeStruct((total.shape[1] + TAIL, NZ * columns), jnp.bfloat16)
    return pl.pallas_call(
        functools.partial(finish_kernel, plan, len(rows)),
        out_shape=[done] * NY,
        in_specs=[SMEM] + [VMEM] * (3 + len(rows)),
        out_specs=[VMEM] * NY,
        scratch_shapes=[
            pltpu.VMEM((weight.shape[0], columns), jnp.float32),
            pltpu.VMEM((NY, total.shape[1], NZ * columns), jnp.float32),
        ],
        compiler_params=pltpu.CompilerParams(vmem_limit_bytes=16 * 2**20),
        cost_estimate=CHEAP,
    )(at, total, mask, weight, *rows)


def rows_kernel(n, at_ref, *refs):
    g_refs, (out_ref, arrived) = refs[:n], refs[n:]
    count, columns = out_ref.shape[0], g_refs[0].shape[1]
    start = pl.multiple_of(at_ref[1] * count, 64)
    copies = [
        pltpu.make_async_copy(
            ref.at[pl.ds(start, count)], out_ref.at[:, j * columns : (j + 1) * columns], arrived.at[j]
        )
        for j, ref in enumerate(g_refs)
    ]
    for copy in copies:
        copy.start()
    for copy in copies:
        copy.wait()


def rows_of(at, g, count):
    return pl.pallas_call(
        functools.partial(rows_kernel, len(g)),
        out_shape=jax.ShapeDtypeStruct((count, len(g) * g[0].shape[1]), g[0].dtype),
        in_specs=[SMEM] + [ANY] * len(g),
        out_specs=VMEM,
        scratch_shapes=[pltpu.SemaphoreType.DMA((len(g),))],
        compiler_params=pltpu.CompilerParams(vmem_limit_bytes=4 * 2**20),
        cost_estimate=CHEAP,
    )(at, *g)


def place_kernel(at_ref, *refs):
    *piece_refs, out_ref, bmat_ref = refs
    _, width, columns = out_ref.shape
    bmat = 0.0
    for k, piece_ref in enumerate(piece_refs):
        owner = lax.rem(at_ref[2] + NY - offset_at(k, at_ref[3]), NY)
        for j, e in enumerate(ORDER):
            slot = lax.rem(at_ref[1] + e, NZ) * NY + owner
            out_ref[slot] = piece_ref[:width, j * columns : (j + 1) * columns]
        tail = piece_ref[width:, :columns].astype(jnp.float32)
        bmat = bmat + tail.sum(0, keepdims=True)
    bmat_ref[...] = jnp.broadcast_to(bmat, bmat_ref.shape)


def place(at, pieces, columns):
    width = pieces[0].shape[0] - TAIL
    return pl.pallas_call(
        place_kernel,
        out_shape=[
            jax.ShapeDtypeStruct((NZ * NY, width, columns), jnp.bfloat16),
            jax.ShapeDtypeStruct((NZ * NX * NC, columns), jnp.float32),
        ],
        in_specs=[SMEM] + [VMEM] * len(pieces),
        out_specs=[VMEM] * 2,
        compiler_params=pltpu.CompilerParams(vmem_limit_bytes=8 * 2**20),
        cost_estimate=CHEAP,
    )(at, *pieces)


def on_device(geminal, fock_matrix, slot_occupied_pair, slot_column_block, slot_live):
    n_fock, _, width, panel_rows = fock_matrix.shape
    columns = geminal.shape[2]
    n_slots = NZ * NY
    z, y, x = lax.axis_index("z"), lax.axis_index("y"), lax.axis_index("x")
    at = jnp.stack([lax.axis_index("c"), z, y, x])
    normalizer = 1.0 / (panel_rows * n_fock * columns)

    own = fock_matrix.reshape(NX, NC, width, panel_rows)
    low, high = split(own)
    g, low, high = lax.optimization_barrier((geminal[0], low, high))
    from_left, from_right = shift_y(low, 1), shift_y(high, -1)
    to_right, to_left = join(low, high, from_left, from_right)
    after_left, after_right = shift_y(to_right, 1), shift_y(to_left, -1)
    f_arrays = [own, from_left, from_right, after_left, after_right]
    f_blocks = (((0, None),), ((1, None), (2, None)), ((4, 0), (3, 1)), ((3, 0), (4, 1)))

    slots = {0: g}
    slots[1], slots[7] = shift_z(slots[0], -1), shift_z(slots[0], 1)
    slots[2], slots[6] = shift_z(slots[1], -1), shift_z(slots[7], 1)
    slots[3], slots[5] = shift_z(slots[2], -1), shift_z(slots[6], 1)

    weight, mask = facts(at, slot_occupied_pair, slot_column_block, slot_live, normalizer, columns)

    def start(plan, order, arrays):
        plan = tuple((f_blocks[j], order.index(es[0]), order.index(es[0]) + len(es)) for j, es in plan)
        away, keep = products(plan, at, arrays, [slots[e] for e in order])
        return swap_core(away), keep

    def spread(total):
        return lax.all_to_all(total, "x", 0, 0)

    def places(plan):
        return tuple((j, tuple(ORDER.index(e) for e in es)) for j, es in plan)

    first = lax.optimization_barrier((*f_arrays[:3], to_right, to_left))[:3]
    recv, keep = start(FIRST, NEAR, list(first))
    packed = pack(keep, recv)
    slots[4] = shift_z(slots[5], 1)

    rows = [rows_of(at, [slots[e] for e in ORDER], NY * width)]
    rows.append(shift_y(rows[0], -1))
    rows.append(shift_y(rows[1], -1))

    rows[0], *f_arrays = lax.optimization_barrier((rows[0], *f_arrays))
    recv, keep = start(SECOND, ORDER, f_arrays)
    total = spread(pack(keep, recv, (packed,)))
    done = finish(places(FIRST + SECOND), at, total, mask, weight, rows)
    out, bmat = place(at, [to_owner(v, j) for j, v in enumerate(done)], columns)
    bmat = lax.all_to_all(bmat, ("z", "x", "c"), 0, 0, tiled=True)
    return out, bmat[:, :4].sum(0).reshape(2, 2)


def solution(mesh):
    mesh = Mesh(mesh.devices.reshape(NZ, NY, NX, NC), ("z", "y", "x", "c"))
    pair, fock = ("z", "y"), ("x", "c")
    return jax.shard_map(
        on_device,
        mesh=mesh,
        in_specs=(P(pair, fock, None), P(None, pair, None, fock), P(), P(), P()),
        out_specs=(P(None, fock + pair, None), P()),
        check_vma=False,
    )
```

```python
import functools

import jax
import jax.numpy as jnp
from jax import lax
from jax.experimental import pallas as pl
from jax.experimental.pallas import tpu as pltpu
from jax.sharding import Mesh
from jax.sharding import PartitionSpec as P

HIGHEST = lax.Precision.HIGHEST
NZ, NY, NX, NC = 8, 4, 4, 2
VMEM = pl.BlockSpec(memory_space=pltpu.VMEM)
SMEM = pl.BlockSpec(memory_space=pltpu.SMEM)
ANY = pl.BlockSpec(memory_space=pl.ANY)
TAIL = 16
CHEAP = pl.CostEstimate(flops=1, bytes_accessed=1, transcendentals=0)

NEAR, FAR = (0, 1, 7, 2, 6), (3, 5, 4)
ORDER = NEAR + FAR
FIRST = ((0, NEAR), (1, NEAR))
SECOND = ((0, FAR), (1, FAR), (2, ORDER), (3, ORDER))


def offset(j, x):
    return (0, -1, 1, 2)[j] if x < NX // 2 else (0, 1, -1, 2)[j]


def offset_at(j, x):
    near, far = jnp.where(x < NX // 2, NY - 1, 1), jnp.where(x < NX // 2, 1, NY - 1)
    return (0, near, far, 2)[j]


def shift_z(v, s):
    return lax.ppermute(v, "z", [(z, (z + s) % NZ) for z in range(NZ)])


def shift_y(v, s):
    return lax.ppermute(v, "y", [(y, (y + s) % NY) for y in range(NY)])


def to_owner(v, j):
    moves = []
    for y in range(NY):
        for x in range(NX):
            moves.append((y * NX + x, (y + offset(j, x)) % NY * NX + x))
    return lax.ppermute(v, ("y", "x"), moves) if j else v


def swap_core(v):
    return lax.ppermute(v, "c", [(0, 1), (1, 0)])


def split_kernel(own_ref, low_ref, high_ref):
    half = own_ref.shape[0] // 2
    low_ref[...] = own_ref[:half]
    high_ref[...] = own_ref[half:]


def split(own):
    half = jax.ShapeDtypeStruct((own.shape[0] // 2,) + own.shape[1:], own.dtype)
    return pl.pallas_call(
        split_kernel,
        out_shape=[half, half],
        in_specs=[VMEM],
        out_specs=[VMEM] * 2,
        compiler_params=pltpu.CompilerParams(vmem_limit_bytes=8 * 2**20),
        cost_estimate=CHEAP,
    )(own)


def join_kernel(low_ref, high_ref, left_ref, right_ref, to_right_ref, to_left_ref, arrived):
    half = low_ref.shape[0]
    moves = [
        (left_ref, to_right_ref.at[:half]),
        (right_ref, to_left_ref.at[half:]),
        (high_ref, to_right_ref.at[half:]),
        (low_ref, to_left_ref.at[:half]),
    ]
    copies = [pltpu.make_async_copy(a, b, arrived.at[i]) for i, (a, b) in enumerate(moves)]
    for copy in copies:
        copy.start()
    for copy in copies:
        copy.wait()


def join(low, high, left, right):
    whole = jax.ShapeDtypeStruct((2 * low.shape[0],) + low.shape[1:], low.dtype)
    return pl.pallas_call(
        join_kernel,
        out_shape=[whole, whole],
        in_specs=[ANY] * 4,
        out_specs=[ANY] * 2,
        scratch_shapes=[pltpu.SemaphoreType.DMA((4,))],
        compiler_params=pltpu.CompilerParams(vmem_limit_bytes=4 * 2**20),
        cost_estimate=CHEAP,
    )(low, high, left, right)


def pack_kernel(keep_ref, recv_ref, *refs):
    *before_ref, out_ref = refs
    _, width, total = keep_ref.shape
    columns = 128
    lane = lax.broadcasted_iota(jnp.int32, (width, columns), 1)
    at = 0
    exponents = jnp.zeros((width, columns), jnp.int32)
    for ref in before_ref:
        at = ref.shape[2] - columns
        out_ref[0, :, :at] = ref[0, :, :at]
        exponents = ref[0, :, at:].astype(jnp.int32)
    for u in range(total // columns):
        span = slice(u * columns, (u + 1) * columns)
        value = keep_ref[0, :, span] + recv_ref[0, :, span]
        top = jnp.maximum(jnp.max(jnp.abs(value), axis=1, keepdims=True), 2.0**-110)
        power = jnp.ceil(jnp.log2(top)) - 15.0
        scaled = jnp.clip(jnp.round(value * jnp.exp2(-power)), -32767.0, 32767.0)
        out_ref[0, :, at + u * columns : at + (u + 1) * columns] = scaled.astype(jnp.int32).astype(jnp.int16)
        exponents = jnp.where(lane == at // columns + u, power.astype(jnp.int32), exponents)
    out_ref[0, :, at + total :] = exponents.astype(jnp.int16)


def pack(keep, recv, before=()):
    n, width, total = keep.shape
    columns = total + (before[0].shape[2] if before else 128)

    def spec(v):
        return pl.BlockSpec((1,) + v.shape[1:], lambda t: (t, 0, 0))

    out = jax.ShapeDtypeStruct((n, width, columns), jnp.int16)
    return pl.pallas_call(
        pack_kernel,
        out_shape=out,
        grid=(n,),
        in_specs=[spec(v) for v in (keep, recv, *before)],
        out_specs=spec(out),
        compiler_params=pltpu.CompilerParams(vmem_limit_bytes=8 * 2**20),
        cost_estimate=CHEAP,
    )(keep, recv, *before)


def products_kernel(plan, n_f, n_g, at_ref, *refs):
    f_refs, g_refs = refs[:n_f], refs[n_f : n_f + n_g]
    away_ref, keep_ref, joined = refs[n_f + n_g :]
    columns = g_refs[0].shape[1]
    first_core = at_ref[0] == 0
    for j, ref in enumerate(g_refs):
        joined[:, j * columns : (j + 1) * columns] = ref[...]
    at = 0
    for pieces, lo, hi in plan:
        span = (hi - lo) * columns
        parts = []
        for i, part in pieces:
            n, cores, width, depth = f_refs[i].shape
            value = f_refs[i][...] if part is None else f_refs[i][part * (n // 2) : (part + 1) * (n // 2)]
            parts.append(value.reshape(-1, depth))
        lhs = parts[0] if len(parts) == 1 else jnp.concatenate(parts, axis=0)
        out = jnp.dot(lhs, joined[:, lo * columns : hi * columns], preferred_element_type=jnp.float32)
        out = out.reshape(NX, NC, width, span)
        keep_ref[:, :, at : at + span] = jnp.where(first_core, out[:, 0], out[:, 1])
        away_ref[:, :, at : at + span] = jnp.where(first_core, out[:, 1], out[:, 0])
        at += span


def products(plan, at, f_arrays, g_pieces):
    width, rows = f_arrays[0].shape[2:]
    columns = g_pieces[0].shape[1]
    units = sum(hi - lo for _, lo, hi in plan)
    terms = jax.ShapeDtypeStruct((NX, width, units * columns), jnp.float32)
    return pl.pallas_call(
        functools.partial(products_kernel, plan, len(f_arrays), len(g_pieces)),
        out_shape=[terms, terms],
        in_specs=[SMEM] + [VMEM] * (len(f_arrays) + len(g_pieces)),
        out_specs=[VMEM] * 2,
        scratch_shapes=[pltpu.VMEM((rows, len(g_pieces) * columns), jnp.bfloat16)],
        compiler_params=pltpu.CompilerParams(vmem_limit_bytes=26 * 2**20),
        cost_estimate=CHEAP,
    )(at, *f_arrays, *g_pieces)


def facts_kernel(normalizer, at_ref, pair_ref, block_ref, live_ref, weight_ref, mask_ref):
    columns = mask_ref.shape[1] // NZ
    lane = lax.broadcasted_iota(jnp.int32, (1, weight_ref.shape[1]), 1)
    z, y = at_ref[1], at_ref[2]
    own = [lax.rem(z + e, NZ) * NY + y for e in range(NZ)]
    own = [own[e] for e in ORDER]
    for i, slot in enumerate(own):
        live = jnp.full((1, columns), live_ref[slot].astype(jnp.float32))
        mask_ref[:, i * columns : (i + 1) * columns] = live
    for k in range(NY - 1):
        for i, f in enumerate(ORDER):
            other = lax.rem(z + f, NZ) * NY + lax.rem(y + k, NY)
            for j, slot in enumerate(own):
                alike = (block_ref[other] == block_ref[slot]).astype(jnp.int32)
                value = (alike * live_ref[other] * live_ref[slot]).astype(jnp.float32) * normalizer
                row = jnp.where(lane == 2 * pair_ref[other] + pair_ref[slot], value, 0.0)
                if k == 1:
                    row = row + jnp.where(lane == 2 * pair_ref[slot] + pair_ref[other], value, 0.0)
                n = (k * NZ + i) * NZ + j
                weight_ref[n : n + 1] = row


def facts(at, pair, block, live, normalizer, columns):
    return pl.pallas_call(
        functools.partial(facts_kernel, normalizer),
        out_shape=[
            jax.ShapeDtypeStruct(((NY - 1) * NZ * NZ, 128), jnp.float32),
            jax.ShapeDtypeStruct((1, NZ * columns), jnp.float32),
        ],
        in_specs=[SMEM] * 4,
        out_specs=[VMEM] * 2,
        compiler_params=pltpu.CompilerParams(vmem_limit_bytes=4 * 2**20),
        cost_estimate=CHEAP,
    )(at, pair, block, live)


def finish_kernel(plan, n_rows, at_ref, total_ref, mask_ref, weight_ref, *refs):
    row_refs, done_refs = refs[:n_rows], refs[n_rows : n_rows + NY]
    dots, made = refs[n_rows + NY :]
    n, width, _ = total_ref.shape
    columns = dots.shape[1]
    units = total_ref.shape[2] - columns
    scales = [jnp.exp2(total_ref[t, :, units:].astype(jnp.int32).astype(jnp.float32)) for t in range(n)]
    u = 0
    for j, es in plan:
        for e in es:
            value = 0.0
            for t in range(n):
                term = total_ref[t, :, u * columns : (u + 1) * columns].astype(jnp.int32).astype(jnp.float32)
                value = value + term * scales[t][:, u : u + 1]
            value = value * mask_ref[:, e * columns : (e + 1) * columns]
            value = value.astype(jnp.bfloat16)
            done_refs[j][:width, e * columns : (e + 1) * columns] = value
            made[j, :, e * columns : (e + 1) * columns] = value.astype(jnp.float32)
            u += 1
    starts = [pl.multiple_of(lax.rem(at_ref[2] + offset_at(j, at_ref[3]), NY) * width, 16) for j in range(NY)]
    for k in range(n_rows):
        for f in range(NZ):
            sums = [0.0] * NZ
            for j, start in enumerate(starts):
                row = row_refs[k][pl.ds(start, width), f * columns : (f + 1) * columns].astype(jnp.float32)
                for e in range(NZ):
                    term = row * made[j, :, e * columns : (e + 1) * columns]
                    sums[e] = sums[e] + term.reshape(width // 8, 8, columns).sum(0)
            for e in range(NZ):
                i = (k * NZ + f) * NZ + e
                dots[i : i + 1] = sums[e].sum(0, keepdims=True)
    bmat = (dots[...].sum(1, keepdims=True) * weight_ref[...]).sum(0, keepdims=True)
    row = lax.broadcasted_iota(jnp.int32, (TAIL, columns), 0)
    tail = jnp.zeros((TAIL, columns), jnp.float32)
    for i in range(3):
        part = bmat.astype(jnp.bfloat16).astype(jnp.float32)
        tail = jnp.where(row == i, part, tail)
        bmat = bmat - part
    for done_ref in done_refs:
        done_ref[width:, :columns] = tail.astype(jnp.bfloat16)
        done_ref[width:, columns:] = jnp.zeros((TAIL, (NZ - 1) * columns), jnp.bfloat16)


def finish(plan, at, total, mask, weight, rows):
    columns = rows[0].shape[1] // NZ
    done = jax.ShapeDtypeStruct((total.shape[1] + TAIL, NZ * columns), jnp.bfloat16)
    return pl.pallas_call(
        functools.partial(finish_kernel, plan, len(rows)),
        out_shape=[done] * NY,
        in_specs=[SMEM] + [VMEM] * (3 + len(rows)),
        out_specs=[VMEM] * NY,
        scratch_shapes=[
            pltpu.VMEM((weight.shape[0], columns), jnp.float32),
            pltpu.VMEM((NY, total.shape[1], NZ * columns), jnp.float32),
        ],
        compiler_params=pltpu.CompilerParams(vmem_limit_bytes=16 * 2**20),
        cost_estimate=CHEAP,
    )(at, total, mask, weight, *rows)


def rows_kernel(n, at_ref, *refs):
    g_refs, (out_ref, arrived) = refs[:n], refs[n:]
    count, columns = out_ref.shape[0], g_refs[0].shape[1]
    start = pl.multiple_of(at_ref[1] * count, 64)
    copies = [
        pltpu.make_async_copy(
            ref.at[pl.ds(start, count)], out_ref.at[:, j * columns : (j + 1) * columns], arrived.at[j]
        )
        for j, ref in enumerate(g_refs)
    ]
    for copy in copies:
        copy.start()
    for copy in copies:
        copy.wait()


def rows_of(at, g, count):
    return pl.pallas_call(
        functools.partial(rows_kernel, len(g)),
        out_shape=jax.ShapeDtypeStruct((count, len(g) * g[0].shape[1]), g[0].dtype),
        in_specs=[SMEM] + [ANY] * len(g),
        out_specs=VMEM,
        scratch_shapes=[pltpu.SemaphoreType.DMA((len(g),))],
        compiler_params=pltpu.CompilerParams(vmem_limit_bytes=4 * 2**20),
        cost_estimate=CHEAP,
    )(at, *g)


def place_kernel(at_ref, *refs):
    *piece_refs, out_ref, bmat_ref = refs
    _, width, columns = out_ref.shape
    bmat = 0.0
    for k, piece_ref in enumerate(piece_refs):
        owner = lax.rem(at_ref[2] + NY - offset_at(k, at_ref[3]), NY)
        for j, e in enumerate(ORDER):
            slot = lax.rem(at_ref[1] + e, NZ) * NY + owner
            out_ref[slot] = piece_ref[:width, j * columns : (j + 1) * columns]
        tail = piece_ref[width:, :columns].astype(jnp.float32)
        bmat = bmat + tail.sum(0, keepdims=True)
    bmat_ref[...] = jnp.broadcast_to(bmat, bmat_ref.shape)


def place(at, pieces, columns):
    width = pieces[0].shape[0] - TAIL
    return pl.pallas_call(
        place_kernel,
        out_shape=[
            jax.ShapeDtypeStruct((NZ * NY, width, columns), jnp.bfloat16),
            jax.ShapeDtypeStruct((NZ * NX * NC, columns), jnp.float32),
        ],
        in_specs=[SMEM] + [VMEM] * len(pieces),
        out_specs=[VMEM] * 2,
        compiler_params=pltpu.CompilerParams(vmem_limit_bytes=8 * 2**20),
        cost_estimate=CHEAP,
    )(at, *pieces)


def on_device(geminal, fock_matrix, slot_occupied_pair, slot_column_block, slot_live):
    n_fock, _, width, panel_rows = fock_matrix.shape
    columns = geminal.shape[2]
    n_slots = NZ * NY
    z, y, x = lax.axis_index("z"), lax.axis_index("y"), lax.axis_index("x")
    at = jnp.stack([lax.axis_index("c"), z, y, x])
    normalizer = 1.0 / (panel_rows * n_fock * columns)

    own = fock_matrix.reshape(NX, NC, width, panel_rows)
    low, high = split(own)
    g, low, high = lax.optimization_barrier((geminal[0], low, high))
    from_left, from_right = shift_y(low, 1), shift_y(high, -1)
    to_right, to_left = join(low, high, from_left, from_right)
    after_left, after_right = shift_y(to_right, 1), shift_y(to_left, -1)
    f_arrays = [own, from_left, from_right, after_left, after_right]
    f_blocks = (((0, None),), ((1, None), (2, None)), ((4, 0), (3, 1)), ((3, 0), (4, 1)))

    slots = {0: g}
    slots[1], slots[7] = shift_z(slots[0], -1), shift_z(slots[0], 1)
    slots[2], slots[6] = shift_z(slots[1], -1), shift_z(slots[7], 1)
    slots[3], slots[5] = shift_z(slots[2], -1), shift_z(slots[6], 1)

    weight, mask = facts(at, slot_occupied_pair, slot_column_block, slot_live, normalizer, columns)

    def start(plan, order, arrays):
        plan = tuple((f_blocks[j], order.index(es[0]), order.index(es[0]) + len(es)) for j, es in plan)
        away, keep = products(plan, at, arrays, [slots[e] for e in order])
        return swap_core(away), keep

    def spread(total):
        return lax.all_to_all(total, "x", 0, 0)

    def places(plan):
        return tuple((j, tuple(ORDER.index(e) for e in es)) for j, es in plan)

    first = lax.optimization_barrier((*f_arrays[:3], to_right, to_left))[:3]
    recv, keep = start(FIRST, NEAR, list(first))
    packed = pack(keep, recv)
    slots[4] = shift_z(slots[5], 1)

    rows = [rows_of(at, [slots[e] for e in ORDER], NY * width)]
    rows.append(shift_y(rows[0], -1))
    rows.append(shift_y(rows[0], 2))

    rows[0], *f_arrays = lax.optimization_barrier((rows[0], *f_arrays))
    recv, keep = start(SECOND, ORDER, f_arrays)
    total = spread(pack(keep, recv, (packed,)))
    done = finish(places(FIRST + SECOND), at, total, mask, weight, rows)
    out, bmat = place(at, [to_owner(v, j) for j, v in enumerate(done)], columns)
    bmat = lax.all_to_all(bmat, ("z", "x", "c"), 0, 0, tiled=True)
    return out, bmat[:, :4].sum(0).reshape(2, 2)


def solution(mesh):
    mesh = Mesh(mesh.devices.reshape(NZ, NY, NX, NC), ("z", "y", "x", "c"))
    pair, fock = ("z", "y"), ("x", "c")
    return jax.shard_map(
        on_device,
        mesh=mesh,
        in_specs=(P(pair, fock, None), P(None, pair, None, fock), P(), P(), P()),
        out_specs=(P(None, fock + pair, None), P()),
        check_vma=False,
    )
```

```python
import functools

import jax
import jax.numpy as jnp
from jax import lax
from jax.experimental import pallas as pl
from jax.experimental.pallas import tpu as pltpu
from jax.sharding import Mesh
from jax.sharding import PartitionSpec as P

HIGHEST = lax.Precision.HIGHEST
NZ, NY, NX, NC = 8, 4, 4, 2
VMEM = pl.BlockSpec(memory_space=pltpu.VMEM)
SMEM = pl.BlockSpec(memory_space=pltpu.SMEM)
ANY = pl.BlockSpec(memory_space=pl.ANY)
TAIL = 16
CHEAP = pl.CostEstimate(flops=1, bytes_accessed=1, transcendentals=0)

NEAR, FAR = (0, 1, 7, 2, 6), (3, 5, 4)
ORDER = NEAR + FAR
FIRST = ((0, NEAR), (1, NEAR))
SECOND = ((0, FAR), (1, FAR), (2, ORDER), (3, ORDER))


def offset(j, x):
    return (0, -1, 1, 2)[j] if x < NX // 2 else (0, 1, -1, 2)[j]


def offset_at(j, x):
    near, far = jnp.where(x < NX // 2, NY - 1, 1), jnp.where(x < NX // 2, 1, NY - 1)
    return (0, near, far, 2)[j]


def shift_z(v, s):
    return lax.ppermute(v, "z", [(z, (z + s) % NZ) for z in range(NZ)])


def shift_y(v, s):
    return lax.ppermute(v, "y", [(y, (y + s) % NY) for y in range(NY)])


def to_owner(v, j):
    moves = []
    for y in range(NY):
        for x in range(NX):
            moves.append((y * NX + x, (y + offset(j, x)) % NY * NX + x))
    return lax.ppermute(v, ("y", "x"), moves) if j else v


def swap_core(v):
    return lax.ppermute(v, "c", [(0, 1), (1, 0)])


def split_kernel(own_ref, low_ref, high_ref):
    half = own_ref.shape[0] // 2
    low_ref[...] = own_ref[:half]
    high_ref[...] = own_ref[half:]


def split(own):
    half = jax.ShapeDtypeStruct((own.shape[0] // 2,) + own.shape[1:], own.dtype)
    return pl.pallas_call(
        split_kernel,
        out_shape=[half, half],
        in_specs=[VMEM],
        out_specs=[VMEM] * 2,
        compiler_params=pltpu.CompilerParams(vmem_limit_bytes=8 * 2**20),
        cost_estimate=CHEAP,
    )(own)


def join_kernel(low_ref, high_ref, left_ref, right_ref, to_right_ref, to_left_ref, arrived):
    half = low_ref.shape[0]
    moves = [
        (left_ref, to_right_ref.at[:half]),
        (right_ref, to_left_ref.at[half:]),
        (high_ref, to_right_ref.at[half:]),
        (low_ref, to_left_ref.at[:half]),
    ]
    copies = [pltpu.make_async_copy(a, b, arrived.at[i]) for i, (a, b) in enumerate(moves)]
    for copy in copies:
        copy.start()
    for copy in copies:
        copy.wait()


def join(low, high, left, right):
    whole = jax.ShapeDtypeStruct((2 * low.shape[0],) + low.shape[1:], low.dtype)
    return pl.pallas_call(
        join_kernel,
        out_shape=[whole, whole],
        in_specs=[ANY] * 4,
        out_specs=[ANY] * 2,
        scratch_shapes=[pltpu.SemaphoreType.DMA((4,))],
        compiler_params=pltpu.CompilerParams(vmem_limit_bytes=4 * 2**20),
        cost_estimate=CHEAP,
    )(low, high, left, right)


def pack_kernel(keep_ref, recv_ref, *refs):
    *before_ref, out_ref = refs
    _, width, total = keep_ref.shape
    columns = 128
    lane = lax.broadcasted_iota(jnp.int32, (width, columns), 1)
    at = 0
    exponents = jnp.zeros((width, columns), jnp.int32)
    for ref in before_ref:
        at = ref.shape[2] - columns
        out_ref[0, :, :at] = ref[0, :, :at]
        exponents = ref[0, :, at:].astype(jnp.int32)
    for u in range(total // columns):
        span = slice(u * columns, (u + 1) * columns)
        value = keep_ref[0, :, span] + recv_ref[0, :, span]
        top = jnp.maximum(jnp.max(jnp.abs(value), axis=1, keepdims=True), 2.0**-110)
        power = jnp.ceil(jnp.log2(top)) - 15.0
        scaled = jnp.clip(jnp.round(value * jnp.exp2(-power)), -32767.0, 32767.0)
        out_ref[0, :, at + u * columns : at + (u + 1) * columns] = scaled.astype(jnp.int32).astype(jnp.int16)
        exponents = jnp.where(lane == at // columns + u, power.astype(jnp.int32), exponents)
    out_ref[0, :, at + total :] = exponents.astype(jnp.int16)


def pack(keep, recv, before=()):
    n, width, total = keep.shape
    columns = total + (before[0].shape[2] if before else 128)

    def spec(v):
        return pl.BlockSpec((1,) + v.shape[1:], lambda t: (t, 0, 0))

    out = jax.ShapeDtypeStruct((n, width, columns), jnp.int16)
    return pl.pallas_call(
        pack_kernel,
        out_shape=out,
        grid=(n,),
        in_specs=[spec(v) for v in (keep, recv, *before)],
        out_specs=spec(out),
        compiler_params=pltpu.CompilerParams(vmem_limit_bytes=8 * 2**20),
        cost_estimate=CHEAP,
    )(keep, recv, *before)


def products_kernel(plan, n_f, n_g, at_ref, *refs):
    f_refs, g_refs = refs[:n_f], refs[n_f : n_f + n_g]
    away_ref, keep_ref, joined = refs[n_f + n_g :]
    columns = g_refs[0].shape[1]
    first_core = at_ref[0] == 0
    for j, ref in enumerate(g_refs):
        joined[:, j * columns : (j + 1) * columns] = ref[...]
    at = 0
    for pieces, lo, hi in plan:
        span = (hi - lo) * columns
        parts = []
        for i, part in pieces:
            n, cores, width, depth = f_refs[i].shape
            value = f_refs[i][...] if part is None else f_refs[i][part * (n // 2) : (part + 1) * (n // 2)]
            parts.append(value.reshape(-1, depth))
        lhs = parts[0] if len(parts) == 1 else jnp.concatenate(parts, axis=0)
        out = jnp.dot(lhs, joined[:, lo * columns : hi * columns], preferred_element_type=jnp.float32)
        out = out.reshape(NX, NC, width, span)
        keep_ref[:, :, at : at + span] = jnp.where(first_core, out[:, 0], out[:, 1])
        away_ref[:, :, at : at + span] = jnp.where(first_core, out[:, 1], out[:, 0])
        at += span


def products(plan, at, f_arrays, g_pieces):
    width, rows = f_arrays[0].shape[2:]
    columns = g_pieces[0].shape[1]
    units = sum(hi - lo for _, lo, hi in plan)
    terms = jax.ShapeDtypeStruct((NX, width, units * columns), jnp.float32)
    return pl.pallas_call(
        functools.partial(products_kernel, plan, len(f_arrays), len(g_pieces)),
        out_shape=[terms, terms],
        in_specs=[SMEM] + [VMEM] * (len(f_arrays) + len(g_pieces)),
        out_specs=[VMEM] * 2,
        scratch_shapes=[pltpu.VMEM((rows, len(g_pieces) * columns), jnp.bfloat16)],
        compiler_params=pltpu.CompilerParams(vmem_limit_bytes=26 * 2**20),
        cost_estimate=CHEAP,
    )(at, *f_arrays, *g_pieces)


def facts_kernel(normalizer, at_ref, pair_ref, block_ref, live_ref, weight_ref, mask_ref):
    columns = mask_ref.shape[1] // NZ
    lane = lax.broadcasted_iota(jnp.int32, (1, weight_ref.shape[1]), 1)
    z, y = at_ref[1], at_ref[2]
    own = [lax.rem(z + e, NZ) * NY + y for e in range(NZ)]
    own = [own[e] for e in ORDER]
    for i, slot in enumerate(own):
        live = jnp.full((1, columns), live_ref[slot].astype(jnp.float32))
        mask_ref[:, i * columns : (i + 1) * columns] = live
    for k in range(NY - 1):
        for i, f in enumerate(ORDER):
            other = lax.rem(z + f, NZ) * NY + lax.rem(y + k, NY)
            for j, slot in enumerate(own):
                alike = (block_ref[other] == block_ref[slot]).astype(jnp.int32)
                value = (alike * live_ref[other] * live_ref[slot]).astype(jnp.float32) * normalizer
                row = jnp.where(lane == 2 * pair_ref[other] + pair_ref[slot], value, 0.0)
                if k == 1:
                    row = row + jnp.where(lane == 2 * pair_ref[slot] + pair_ref[other], value, 0.0)
                n = (k * NZ + i) * NZ + j
                weight_ref[n : n + 1] = row


def facts(at, pair, block, live, normalizer, columns):
    return pl.pallas_call(
        functools.partial(facts_kernel, normalizer),
        out_shape=[
            jax.ShapeDtypeStruct(((NY - 1) * NZ * NZ, 128), jnp.float32),
            jax.ShapeDtypeStruct((1, NZ * columns), jnp.float32),
        ],
        in_specs=[SMEM] * 4,
        out_specs=[VMEM] * 2,
        compiler_params=pltpu.CompilerParams(vmem_limit_bytes=4 * 2**20),
        cost_estimate=CHEAP,
    )(at, pair, block, live)


def finish_kernel(plan, n_rows, at_ref, total_ref, mask_ref, weight_ref, *refs):
    row_refs, done_refs = refs[:n_rows], refs[n_rows : n_rows + NY]
    dots, made = refs[n_rows + NY :]
    n, width, _ = total_ref.shape
    columns = dots.shape[1]
    units = total_ref.shape[2] - columns
    scales = [jnp.exp2(total_ref[t, :, units:].astype(jnp.int32).astype(jnp.float32)) for t in range(n)]
    u = 0
    for j, es in plan:
        for e in es:
            value = 0.0
            for t in range(n):
                term = total_ref[t, :, u * columns : (u + 1) * columns].astype(jnp.int32).astype(jnp.float32)
                value = value + term * scales[t][:, u : u + 1]
            value = value * mask_ref[:, e * columns : (e + 1) * columns]
            value = value.astype(jnp.bfloat16)
            done_refs[j][:width, e * columns : (e + 1) * columns] = value
            made[j, :, e * columns : (e + 1) * columns] = value.astype(jnp.float32)
            u += 1
    starts = [pl.multiple_of(lax.rem(at_ref[2] + offset_at(j, at_ref[3]), NY) * width, 16) for j in range(NY)]
    for k in range(n_rows):
        for f in range(NZ):
            sums = [0.0] * NZ
            for j, start in enumerate(starts):
                row = row_refs[k][pl.ds(start, width), f * columns : (f + 1) * columns].astype(jnp.float32)
                for e in range(NZ):
                    term = row * made[j, :, e * columns : (e + 1) * columns]
                    sums[e] = sums[e] + term.reshape(width // 8, 8, columns).sum(0)
            for e in range(NZ):
                i = (k * NZ + f) * NZ + e
                dots[i : i + 1] = sums[e].sum(0, keepdims=True)
    bmat = (dots[...].sum(1, keepdims=True) * weight_ref[...]).sum(0, keepdims=True)
    row = lax.broadcasted_iota(jnp.int32, (TAIL, columns), 0)
    tail = jnp.zeros((TAIL, columns), jnp.float32)
    for i in range(3):
        part = bmat.astype(jnp.bfloat16).astype(jnp.float32)
        tail = jnp.where(row == i, part, tail)
        bmat = bmat - part
    for done_ref in done_refs:
        done_ref[width:, :columns] = tail.astype(jnp.bfloat16)
        done_ref[width:, columns:] = jnp.zeros((TAIL, (NZ - 1) * columns), jnp.bfloat16)


def finish(plan, at, total, mask, weight, rows):
    columns = rows[0].shape[1] // NZ
    done = jax.ShapeDtypeStruct((total.shape[1] + TAIL, NZ * columns), jnp.bfloat16)
    return pl.pallas_call(
        functools.partial(finish_kernel, plan, len(rows)),
        out_shape=[done] * NY,
        in_specs=[SMEM] + [VMEM] * (3 + len(rows)),
        out_specs=[VMEM] * NY,
        scratch_shapes=[
            pltpu.VMEM((weight.shape[0], columns), jnp.float32),
            pltpu.VMEM((NY, total.shape[1], NZ * columns), jnp.float32),
        ],
        compiler_params=pltpu.CompilerParams(vmem_limit_bytes=16 * 2**20),
        cost_estimate=CHEAP,
    )(at, total, mask, weight, *rows)


def rows_kernel(n, at_ref, *refs):
    g_refs, (out_ref, arrived) = refs[:n], refs[n:]
    count, columns = out_ref.shape[0], g_refs[0].shape[1]
    start = pl.multiple_of(at_ref[1] * count, 64)
    copies = [
        pltpu.make_async_copy(
            ref.at[pl.ds(start, count)], out_ref.at[:, j * columns : (j + 1) * columns], arrived.at[j]
        )
        for j, ref in enumerate(g_refs)
    ]
    for copy in copies:
        copy.start()
    for copy in copies:
        copy.wait()


def rows_of(at, g, count):
    return pl.pallas_call(
        functools.partial(rows_kernel, len(g)),
        out_shape=jax.ShapeDtypeStruct((count, len(g) * g[0].shape[1]), g[0].dtype),
        in_specs=[SMEM] + [ANY] * len(g),
        out_specs=VMEM,
        scratch_shapes=[pltpu.SemaphoreType.DMA((len(g),))],
        compiler_params=pltpu.CompilerParams(vmem_limit_bytes=4 * 2**20),
        cost_estimate=CHEAP,
    )(at, *g)


def place_kernel(at_ref, *refs):
    *piece_refs, out_ref = refs
    _, width, columns = out_ref.shape
    for k, piece_ref in enumerate(piece_refs):
        owner = lax.rem(at_ref[2] + NY - offset_at(k, at_ref[3]), NY)
        for j, e in enumerate(ORDER):
            slot = lax.rem(at_ref[1] + e, NZ) * NY + owner
            out_ref[slot] = piece_ref[:width, j * columns : (j + 1) * columns]


def place(at, pieces, columns):
    width = pieces[0].shape[0] - TAIL
    return pl.pallas_call(
        place_kernel,
        out_shape=jax.ShapeDtypeStruct((NZ * NY, width, columns), jnp.bfloat16),
        in_specs=[SMEM] + [VMEM] * len(pieces),
        out_specs=VMEM,
        compiler_params=pltpu.CompilerParams(vmem_limit_bytes=8 * 2**20),
        cost_estimate=CHEAP,
    )(at, *pieces)


def terms_kernel(*refs):
    *piece_refs, bmat_ref, held, arrived = refs
    width, columns = held.shape[1:]
    copies = [
        pltpu.make_async_copy(ref.at[ref.shape[0] - width :, :columns], held.at[i], arrived.at[i])
        for i, ref in enumerate(piece_refs)
    ]
    for copy in copies:
        copy.start()
    for copy in copies:
        copy.wait()
    bmat = held[...].astype(jnp.float32).sum(0).sum(0, keepdims=True)
    bmat_ref[...] = jnp.broadcast_to(bmat, bmat_ref.shape)


def terms(pieces, columns):
    return pl.pallas_call(
        terms_kernel,
        out_shape=jax.ShapeDtypeStruct((NZ * NX * NC, columns), jnp.float32),
        in_specs=[ANY] * len(pieces),
        out_specs=VMEM,
        scratch_shapes=[
            pltpu.VMEM((len(pieces), TAIL, columns), jnp.bfloat16),
            pltpu.SemaphoreType.DMA((len(pieces),)),
        ],
        compiler_params=pltpu.CompilerParams(vmem_limit_bytes=4 * 2**20),
        cost_estimate=CHEAP,
    )(*pieces)


def on_device(geminal, fock_matrix, slot_occupied_pair, slot_column_block, slot_live):
    n_fock, _, width, panel_rows = fock_matrix.shape
    columns = geminal.shape[2]
    n_slots = NZ * NY
    z, y, x = lax.axis_index("z"), lax.axis_index("y"), lax.axis_index("x")
    at = jnp.stack([lax.axis_index("c"), z, y, x])
    normalizer = 1.0 / (panel_rows * n_fock * columns)

    own = fock_matrix.reshape(NX, NC, width, panel_rows)
    low, high = split(own)
    g, low, high = lax.optimization_barrier((geminal[0], low, high))
    from_left, from_right = shift_y(low, 1), shift_y(high, -1)
    to_right, to_left = join(low, high, from_left, from_right)
    after_left, after_right = shift_y(to_right, 1), shift_y(to_left, -1)
    f_arrays = [own, from_left, from_right, after_left, after_right]
    f_blocks = (((0, None),), ((1, None), (2, None)), ((4, 0), (3, 1)), ((3, 0), (4, 1)))

    slots = {0: g}
    slots[1], slots[7] = shift_z(slots[0], -1), shift_z(slots[0], 1)
    slots[2], slots[6] = shift_z(slots[1], -1), shift_z(slots[7], 1)
    slots[3], slots[5] = shift_z(slots[2], -1), shift_z(slots[6], 1)

    weight, mask = facts(at, slot_occupied_pair, slot_column_block, slot_live, normalizer, columns)

    def start(plan, order, arrays):
        plan = tuple((f_blocks[j], order.index(es[0]), order.index(es[0]) + len(es)) for j, es in plan)
        away, keep = products(plan, at, arrays, [slots[e] for e in order])
        return swap_core(away), keep

    def spread(total):
        return lax.all_to_all(total, "x", 0, 0)

    def places(plan):
        return tuple((j, tuple(ORDER.index(e) for e in es)) for j, es in plan)

    first = lax.optimization_barrier((*f_arrays[:3], to_right, to_left))[:3]
    recv, keep = start(FIRST, NEAR, list(first))
    packed = pack(keep, recv)
    slots[4] = shift_z(slots[5], 1)

    rows = [rows_of(at, [slots[e] for e in ORDER], NY * width)]
    rows.append(shift_y(rows[0], -1))
    rows.append(shift_y(rows[0], 2))

    rows[0], *f_arrays = lax.optimization_barrier((rows[0], *f_arrays))
    recv, keep = start(SECOND, ORDER, f_arrays)
    total = spread(pack(keep, recv, (packed,)))
    done = finish(places(FIRST + SECOND), at, total, mask, weight, rows)
    pieces = [to_owner(v, j) for j, v in enumerate(done)]
    out = place(at, pieces, columns)
    bmat = lax.all_to_all(terms(pieces, columns), ("z", "x", "c"), 0, 0, tiled=True)
    return out, bmat[:, :4].sum(0).reshape(2, 2)


def solution(mesh):
    mesh = Mesh(mesh.devices.reshape(NZ, NY, NX, NC), ("z", "y", "x", "c"))
    pair, fock = ("z", "y"), ("x", "c")
    return jax.shard_map(
        on_device,
        mesh=mesh,
        in_specs=(P(pair, fock, None), P(None, pair, None, fock), P(), P(), P()),
        out_specs=(P(None, fock + pair, None), P()),
        check_vma=False,
    )
```
